768 devices in a mesh: blk: 384 (over z, y_lo, x, core), grp: 2 (over y_hi).
Axes of the slice: x: 4, y: 8 (y_hi: 2, y_lo: 4; y = y_hi * 4 + y_lo), z: 12, core: 2. Of those that a mesh axis runs over, the one named last changes fastest.
Arguments:
- image_embed: bfloat16 [98304, 1152], P(('blk', 'grp')), may hold values from -6 to 6
- text_embed: bfloat16 [98304, 1152], P(('blk', 'grp')), may hold values from -6 to 6
- pair_labels: int32 [98304], P('blk'), may hold values from 0 to 98303, as said below
- logit_scale: float32 [1], replicated, may hold values from 1 to 4
- logit_bias: float32 [1], replicated, may hold values from -3 to -1
Outputs:
- mean_loss: float32 [], replicated
- grad_image: float32 [98304, 1152], P(('blk', 'grp'))
- grad_text: float32 [98304, 1152], P(('blk', 'grp'))
The draws below stay inside these ranges and needn't reach their ends.
Inputs may be any that keep to these rules, and one draw needn't show every extreme that they name: `pair_labels`: the text row that matches an image row lies in a block that is 0 to 3 blocks before the image row's own block, counted around the 384 blocks; several image rows may match one text row.
All inputs are finite; a program needn't handle non-finite values.
Results may differ from the reference program's by a relative error of at most 0.0026.
Values may be sent and summed in bfloat16 or wider, within the bound.
A program may use at most 32 MiB of HBM per device.

```python
import math
import jax
import jax.numpy as jnp
from jax import lax

D = 1152
ROWS_DEV = 128
STEPS = 4
BLOCKS = 384
BLOCK_ROWS = 256
IMAGES = 98304
N_BLK = 384
N_GRP = 2


def draw_pair_labels(key, part):
    key = jax.random.fold_in(key, 7)
    first_key, second_key = jax.random.split(key)
    row_index = jnp.arange(IMAGES, dtype=jnp.int32)
    home_block = row_index // BLOCK_ROWS
    back_steps = jax.random.randint(first_key, (IMAGES,), 0, STEPS, dtype=jnp.int32)
    within_block = jax.random.randint(second_key, (IMAGES,), 0, BLOCK_ROWS, dtype=jnp.int32)
    labels = (home_block - back_steps) % BLOCKS * BLOCK_ROWS + within_block
    labels = labels.at[0].set(jnp.int32(IMAGES - 1))
    labels = labels.at[1].set(jnp.int32(0))
    return labels


def block_scale(key, extent, cuts, low, top_value):
    level, own = 1.0, jax.random.fold_in(key, 6)
    for position, parts in cuts:
        heights = jnp.exp(jax.random.uniform(jax.random.fold_in(own, position), (parts,), jnp.float32, low / len(cuts), top_value / len(cuts)))
        level = level * jnp.repeat(heights, extent[position] // parts).reshape([-1 if axis == position else 1 for axis in range(len(extent))])
    return level


def centred(key, shape, spread, bound, cuts=(), kind=jnp.bfloat16):
    entries = jax.random.normal(key, shape, jnp.float32) * spread
    if len(cuts) > 0:
        entries = block_scale(key, shape, cuts, -0.22, 0.18) * entries
    return jnp.clip(entries, min=-bound, max=bound).astype(kind)


def setup_inputs(seed: int = 0) -> dict:
    arg_keys = jax.random.split(jax.random.key(seed), 6)
    image_embed = centred(arg_keys[0], (IMAGES, D), 1.0, 6.0, ((0, 768),))
    text_embed = centred(arg_keys[1], (IMAGES, D), 1.0, 6.0, ((0, 768),))
    pair_labels = draw_pair_labels(jax.random.fold_in(arg_keys[5], 71), 0)
    logit_scale = jnp.clip(jnp.exp(jax.random.uniform(arg_keys[3], (1,), jnp.float32, math.log(1.0), math.log(4.0))), 1.0, 4.0)
    logit_bias = jnp.clip(jax.random.uniform(arg_keys[4], (1,), jnp.float32, -3.0, -1.0), -3.0, -1.0)
    return {"image_embed": image_embed, "text_embed": text_embed, "pair_labels": pair_labels, "logit_scale": logit_scale, "logit_bias": logit_bias}


def pair_tile(image_rows, row_labels, text_rows, text_ids, factor, shift_bias):
    logits = factor * jnp.dot(image_rows, text_rows.T, preferred_element_type=jnp.float32) + shift_bias
    signs = jnp.where(row_labels[:, None] == text_ids[None, :], 1.0, -1.0).astype(logits.dtype)
    weights = (-signs * jax.nn.sigmoid(-signs * logits)).astype(jnp.bfloat16)
    return (weights, -jnp.sum(jax.nn.log_sigmoid(signs * logits)))

def reference(image_embed, text_embed, pair_labels, logit_scale, logit_bias):
    width = image_embed.shape[1]
    block_rows = ROWS_DEV * N_GRP
    block_count = N_BLK
    images = image_embed.reshape(block_count, block_rows, width)
    texts = text_embed.reshape(block_count, block_rows, width)
    label_blocks = pair_labels.reshape(block_count, block_rows)
    factor = logit_scale[0] / math.sqrt(width)
    shift_bias = logit_bias[0]
    offsets = jnp.arange(block_rows, dtype=jnp.int32)

    def image_side(block_index):
        total = jnp.zeros((block_rows, width), jnp.float32)
        loss_part = jnp.zeros((), jnp.float32)
        for loop_step in range(STEPS):
            source = (block_index - loop_step) % block_count
            text_rows = texts[source]
            weights, part = pair_tile(images[block_index], label_blocks[block_index], text_rows, source * block_rows + offsets, factor, shift_bias)
            total = total + factor * jnp.dot(weights, text_rows, preferred_element_type=jnp.float32)
            loss_part = loss_part + part
        return (total, loss_part)

    def text_side(block_index):
        total = jnp.zeros((block_rows, width), jnp.float32)
        for loop_step in range(STEPS):
            target = (block_index + loop_step) % block_count
            image_rows = images[target]
            weights, part = pair_tile(image_rows, label_blocks[target], texts[block_index], block_index * block_rows + offsets, factor, shift_bias)
            total = total + factor * jnp.dot(weights.T, image_rows, preferred_element_type=jnp.float32)
        return total
    block_list = jnp.arange(block_count, dtype=jnp.int32)
    image_grads, losses = lax.map(image_side, block_list)
    text_grads = lax.map(text_side, block_list)
    mean_loss = jnp.sum(losses) / (block_count * block_rows)
    return (mean_loss, image_grads.reshape(-1, width), text_grads.reshape(-1, width))
```

```python
import math

import jax
import jax.numpy as jnp
from jax import lax
from jax.experimental import pallas as pl
from jax.experimental.pallas import tpu as pltpu
from jax.sharding import PartitionSpec as P

STEPS = 4
NT = (((1,), (1,)), ((), ()))
TN = (((0,), (0,)), ((), ()))


def rem_copy(src, dst, send, recv, dev):
    return pltpu.make_async_remote_copy(
        src_ref=src, dst_ref=dst, send_sem=send, recv_sem=recv, device_id=dev,
        device_id_type=pl.DeviceIdType.MESH)


def kernel(image_hbm, text_hbm, labels_hbm, scale_ref, bias_ref,
           loss_ref, grad_image_ref, grad_text_ref,
           images, texts, labels, weights, out_other, in_other, mate_out, mate_in, ext_out, ext_in,
           sum_out, sum_in, loss_xc, loss_y, loss_z, loss_q,
           send, recv, local, xc_send, xc_recv, y_send, y_recv, z_send, z_recv, q_send, q_recv, token):
    rows, width = image_hbm.shape
    blocks = lax.axis_size("blk")
    b = lax.axis_index("blk")
    g = lax.axis_index("grp")
    core = b % 2
    x = (b // 2) % 4
    y = g * 4 + (b // 8) % 4
    z = b // 32
    zq = z // 4
    zr = z % 4

    def at(k):
        return (lax.rem(b + k + blocks, blocks), g)

    def place(x, y, z, core):
        return (((z * 4 + y % 4) * 4 + x) * 2 + core, y // 4)

    partner = (b, 1 - g)
    mate = (b + 1 - 2 * core, g)
    xc_me = x * 2 + core
    xc_peers = [lax.rem(xc_me + i, 8) for i in range(1, 8)]
    y_peers = [lax.rem(y + i, 8) for i in range(1, 8)]
    r_peers = [lax.rem(zr + i, 4) for i in range(1, 4)]
    q_peers = [lax.rem(zq + i, 3) for i in range(1, 3)]
    xc_devs = [place(p // 2, y, z, p % 2) for p in xc_peers]
    y_devs = [place(x, p, z, core) for p in y_peers]
    r_devs = [place(x, y, zq * 4 + p, core) for p in r_peers]
    q_devs = [place(x, y, p * 4 + zr, core) for p in q_peers]

    barrier = pltpu.get_barrier_semaphore()
    greeted = [at(1), at(-1), at(3), at(-3), partner] + xc_devs + y_devs + r_devs
    for dev in greeted:
        pl.semaphore_signal(barrier, inc=1, device_id=dev)

    @pl.when(zq == 1)
    def _():
        for dev in q_devs:
            pl.semaphore_signal(barrier, inc=1, device_id=dev)

    @pl.when(zq != 1)
    def _():
        pl.semaphore_signal(barrier, inc=1, device_id=place(x, y, 4 + zr, core))

    local_copies = [
        pltpu.make_async_copy(image_hbm, images.at[pl.ds(0, rows)], local.at[0]),
        pltpu.make_async_copy(text_hbm, texts.at[0], local.at[1]),
        pltpu.make_async_copy(labels_hbm, labels, local.at[2]),
    ]
    for c in local_copies:
        c.start()

    @pl.when(zq == 1)
    def _():
        pl.semaphore_wait(barrier, len(greeted) + 2)

    @pl.when(zq != 1)
    def _():
        pl.semaphore_wait(barrier, len(greeted) + 1)

    text_1 = rem_copy(text_hbm, texts.at[1], send.at[1], recv.at[1], at(1))
    text_3 = rem_copy(text_hbm, texts.at[3], send.at[3], recv.at[3], at(3))
    image_over = rem_copy(image_hbm, images.at[pl.ds(rows, rows)], send.at[0], recv.at[0], partner)
    text_1.start()
    text_3.start()
    image_over.start()

    @pl.when(zq == 1)
    def _():
        for dev in q_devs:
            pl.semaphore_signal(token, inc=1, device_id=dev)

    factor = scale_ref[0] / math.sqrt(width)
    shift_bias = bias_ref[0]
    for c in local_copies:
        c.wait()
    positions = lax.broadcasted_iota(jnp.int32, (rows, rows), 0) + g * rows

    def tile(slot, half, image_rows):
        logits = factor * lax.dot_general(
            texts[slot], image_rows, NT, preferred_element_type=jnp.float32) + shift_bias
        source = lax.rem(b - slot + blocks, blocks)
        row_labels = labels[pl.ds(g if half == 0 else 1 - g, 1), :]
        match = (positions + source * (2 * rows)) == row_labels
        turned = jnp.where(match, -logits, logits)
        small = jnp.exp(-jnp.abs(turned))
        sig = jnp.where(turned >= 0, 1.0, small) / (1.0 + small)
        weights[slot, :, pl.ds(half * rows, rows)] = jnp.where(match, -sig, sig).astype(jnp.bfloat16)
        terms = jnp.maximum(turned, 0.0) + jnp.log1p(small)
        return jnp.sum(terms.reshape(rows // 8, 8, rows), axis=0)

    own = images[pl.ds(0, rows)]
    total = tile(0, 0, own)
    near, far = 1 + 2 * core, 3 - 2 * core
    rem_copy(text_hbm, texts.at[near], send.at[near], recv.at[near], mate).wait_recv()
    forward = rem_copy(texts.at[near], texts.at[2], send.at[2], recv.at[2], mate)
    forward.start()
    total += tile(near, 0, own)
    rem_copy(text_hbm, texts.at[far], send.at[far], recv.at[far], mate).wait_recv()
    total += tile(far, 0, own)
    forward.wait_recv()
    total += tile(2, 0, own)
    all_texts = texts[...].reshape(STEPS * rows, width)
    acc = lax.dot_general(weights[:, :, pl.ds(0, rows)].reshape(STEPS * rows, rows), all_texts, TN,
                          preferred_element_type=jnp.float32)
    grad_image_ref[...] = acc

    image_over.wait_recv()
    other = images[pl.ds(rows, rows)]
    for slot in range(STEPS):
        total += tile(slot, 1, other)
    out_other[...] = lax.dot_general(
        weights[:, :, pl.ds(rows, rows)].reshape(STEPS * rows, rows), all_texts, TN,
        preferred_element_type=jnp.float32).astype(jnp.bfloat16)
    back = rem_copy(out_other, in_other, send.at[4], recv.at[4], partner)
    back.start()

    loss_xc[xc_me] = total
    xc_copies = [rem_copy(loss_xc.at[xc_me], loss_xc.at[xc_me], xc_send.at[i], xc_recv.at[i], dev)
                 for i, dev in enumerate(xc_devs)]
    for c in xc_copies:
        c.start()

    def partial(slot):
        return jnp.dot(weights[slot], images[...], preferred_element_type=jnp.float32)

    mate_out[...] = partial(2).astype(jnp.bfloat16)
    to_mate = rem_copy(mate_out, mate_in, send.at[5], recv.at[5], mate)
    to_mate.start()
    ext_out[...] = partial(far).astype(jnp.bfloat16)
    to_ext = rem_copy(ext_out, ext_in, send.at[6], recv.at[6], at(2 * core - 3))
    to_ext.start()
    mine = partial(near)
    to_mate.wait_recv()
    sum_out[...] = (mine + mate_in[...].astype(jnp.float32)).astype(jnp.bfloat16)
    to_sum = rem_copy(sum_out, sum_in, send.at[7], recv.at[7], at(-1 - 2 * core))
    to_sum.start()
    grad_text_ref[...] = partial(0)

    def ordered(buffer, count):
        value = buffer[0]
        for i in range(1, count):
            value = value + buffer[i]
        return value

    for c in xc_copies:
        c.wait_recv()
    loss_y[y] = ordered(loss_xc, 8)
    y_copies = [rem_copy(loss_y.at[y], loss_y.at[y], y_send.at[i], y_recv.at[i], dev)
                for i, dev in enumerate(y_devs)]
    for c in y_copies:
        c.start()
    for c in y_copies:
        c.wait_recv()
    loss_z[zr] = ordered(loss_y, 8)
    z_copies = [rem_copy(loss_z.at[zr], loss_z.at[zr], z_send.at[i], z_recv.at[i], dev)
                for i, dev in enumerate(r_devs)]
    for c in z_copies:
        c.start()
    for c in z_copies:
        c.wait_recv()
    loss_q[zq] = ordered(loss_z, 4)

    @pl.when(zq != 1)
    def _():
        pl.semaphore_wait(token, 1)

    q_copies = [rem_copy(loss_q.at[zq], loss_q.at[zq], q_send.at[i], q_recv.at[i], dev)
                for i, dev in enumerate(q_devs)]
    for c in q_copies:
        c.start()

    back.wait_recv()
    grad_image_ref[...] = factor * (grad_image_ref[...] + in_other[...].astype(jnp.float32))
    to_ext.wait_recv()
    to_sum.wait_recv()
    grad_text_ref[...] = factor * (
        grad_text_ref[...] + ext_in[...].astype(jnp.float32) + sum_in[...].astype(jnp.float32))
    for c in q_copies:
        c.wait_recv()
    whole = jnp.sum(jnp.sum(ordered(loss_q, 3), axis=1, keepdims=True), axis=0, keepdims=True)
    loss_ref[...] = whole / (blocks * 2 * rows)
    for c in [text_1, text_3, image_over, forward, back, to_mate, to_ext, to_sum] + xc_copies + y_copies + z_copies + q_copies:
        c.wait_send()


def body(image_embed, text_embed, pair_labels, logit_scale, logit_bias):
    rows, width = image_embed.shape
    shard = pltpu.VMEM((rows, width), jnp.bfloat16)
    dma = pltpu.SemaphoreType.DMA
    tiles = lambda n: pltpu.VMEM((n, 8, 128), jnp.float32)
    any_space = pl.BlockSpec(memory_space=pl.ANY)
    smem = pl.BlockSpec(memory_space=pltpu.SMEM)
    vmem = pl.BlockSpec(memory_space=pltpu.VMEM)
    grad = jax.ShapeDtypeStruct((rows, width), jnp.float32)
    mean_loss, grad_image, grad_text = pl.pallas_call(
        kernel,
        out_shape=(jax.ShapeDtypeStruct((1, 1), jnp.float32), grad, grad),
        in_specs=[any_space, any_space, any_space, smem, smem],
        out_specs=(vmem, vmem, vmem),
        scratch_shapes=[
            pltpu.VMEM((2 * rows, width), jnp.bfloat16),
            pltpu.VMEM((STEPS, rows, width), jnp.bfloat16),
            pltpu.VMEM((2, rows), jnp.int32),
            pltpu.VMEM((STEPS, rows, 2 * rows), jnp.bfloat16),
            shard, shard, shard, shard, shard, shard, shard, shard,
            tiles(8), tiles(8), tiles(4), tiles(3),
            dma((8,)), dma((8,)), dma((3,)),
            dma((7,)), dma((7,)), dma((7,)), dma((7,)), dma((3,)), dma((3,)), dma((2,)), dma((2,)),
            pltpu.SemaphoreType.REGULAR,
        ],
        compiler_params=pltpu.CompilerParams(
            collective_id=0, has_side_effects=True, vmem_limit_bytes=40 * 2**20),
        cost_estimate=pl.CostEstimate(
            flops=6 * 2 * rows * STEPS * rows * width, bytes_accessed=8 * rows * width, transcendentals=0),
        name="band",
    )(image_embed, text_embed, pair_labels.reshape(2, rows), logit_scale, logit_bias)
    return mean_loss.reshape(()), grad_image, grad_text


def solution(mesh):
    in_specs = (P(("blk", "grp"), None), P(("blk", "grp"), None), P("blk"), P(), P())
    out_specs = (P(), P(("blk", "grp"), None), P(("blk", "grp"), None))
    return jax.shard_map(body, mesh=mesh, in_specs=in_specs, out_specs=out_specs, check_vma=False)
```

```python
import math

import jax
import jax.numpy as jnp
from jax import lax
from jax.experimental import pallas as pl
from jax.experimental.pallas import tpu as pltpu
from jax.sharding import PartitionSpec as P

STEPS = 4
CHUNKS = 2
NT = (((1,), (1,)), ((), ()))
TN = (((0,), (0,)), ((), ()))


def rem_copy(src, dst, send, recv, dev):
    return pltpu.make_async_remote_copy(
        src_ref=src, dst_ref=dst, send_sem=send, recv_sem=recv, device_id=dev,
        device_id_type=pl.DeviceIdType.MESH)


def kernel(image_hbm, text_hbm, labels_hbm, scale_ref, bias_ref,
           loss_ref, grad_image_ref, grad_text_ref,
           images, texts, labels, weights, weights_other, relay, out_other, in_other, mate_out, mate_in,
           ext_out, ext_in, sum_out, sum_in, loss_xc, loss_y, loss_z, loss_q,
           send, recv, over_send, over_recv, back_send, back_recv, local, xc_send, xc_recv, y_send, y_recv, z_send, z_recv, q_send, q_recv, token):
    rows, width = image_hbm.shape
    blocks = lax.axis_size("blk")
    b = lax.axis_index("blk")
    g = lax.axis_index("grp")
    core = b % 2
    x = (b // 2) % 4
    y = g * 4 + (b // 8) % 4
    z = b // 32
    zq = z // 4
    zr = z % 4

    def at(k):
        return (lax.rem(b + k + blocks, blocks), g)

    def place(x, y, z, core):
        return (((z * 4 + y % 4) * 4 + x) * 2 + core, y // 4)

    partner = (b, 1 - g)
    mate = (b + 1 - 2 * core, g)
    xc_me = x * 2 + core
    xc_peers = [lax.rem(xc_me + i, 8) for i in range(1, 8)]
    y_peers = [lax.rem(y + i, 8) for i in range(1, 8)]
    r_peers = [lax.rem(zr + i, 4) for i in range(1, 4)]
    q_peers = [lax.rem(zq + i, 3) for i in range(1, 3)]
    xc_devs = [place(p // 2, y, z, p % 2) for p in xc_peers]
    y_devs = [place(x, p, z, core) for p in y_peers]
    r_devs = [place(x, y, zq * 4 + p, core) for p in r_peers]
    q_devs = [place(x, y, p * 4 + zr, core) for p in q_peers]

    barrier = pltpu.get_barrier_semaphore()
    greeted = [at(-k) for k in (1, 2, 3, 8)] + [partner] + xc_devs + y_devs + r_devs
    for dev in greeted:
        pl.semaphore_signal(barrier, inc=1, device_id=dev)

    greeters = len(greeted) + jnp.where(zq == 1, 2, 1)
    for k in (1, 2, 3, 8):
        greeters += jnp.where(b >= k, 1, 0)

        @pl.when(b + k < blocks)
        def _():
            pl.semaphore_signal(barrier, inc=1, device_id=at(k))

    @pl.when(zq == 1)
    def _():
        for dev in q_devs:
            pl.semaphore_signal(barrier, inc=1, device_id=dev)

    @pl.when(zq != 1)
    def _():
        pl.semaphore_signal(barrier, inc=1, device_id=place(x, y, 4 + zr, core))

    local_copies = [
        pltpu.make_async_copy(image_hbm, images.at[pl.ds(0, rows)], local.at[0]),
        pltpu.make_async_copy(text_hbm, texts.at[0], local.at[1]),
        pltpu.make_async_copy(labels_hbm, labels, local.at[2]),
    ]
    for c in local_copies:
        c.start()

    pl.semaphore_wait(barrier, greeters)

    first, last = x == 0, x == 3
    text_1 = rem_copy(text_hbm, texts.at[1], send.at[1], recv.at[1], at(1))
    text_3 = rem_copy(text_hbm, texts.at[3], send.at[3], recv.at[3], at(3))
    text_relay = rem_copy(text_hbm, relay, send.at[3], recv.at[8], at(-5))
    text_1.start()
    direct = ((core == 0) & (x != 3)) | ((core == 1) & (x == 2))
    by_relay = (core == 0) & last

    @pl.when(direct)
    def _():
        text_3.start()

    @pl.when(by_relay)
    def _():
        text_relay.start()

    part = rows // CHUNKS
    over = [rem_copy(image_hbm.at[pl.ds(c * part, part)], images.at[pl.ds(rows + c * part, part)],
                     over_send.at[c], over_recv.at[c], partner) for c in range(CHUNKS)]
    relays_text = (core == 1) & first
    relay_text = rem_copy(relay, texts.at[3], send.at[8], recv.at[3], at(8))
    over[0].start()

    @pl.when(relays_text)
    def _():
        text_relay.wait_recv()
        relay_text.start()

    for c in over[1:]:
        c.start()

    @pl.when(zq == 1)
    def _():
        for dev in q_devs:
            pl.semaphore_signal(token, inc=1, device_id=dev)

    factor = scale_ref[0] / math.sqrt(width)
    shift_bias = bias_ref[0]
    for c in local_copies:
        c.wait()
    own_ids = lax.broadcasted_iota(jnp.int32, (rows, rows), 0) + g * rows
    other_ids = lax.broadcasted_iota(jnp.int32, (rows, rows), 1) + g * rows
    own_labels = labels[pl.ds(g, 1), :]
    other_labels = jnp.broadcast_to(labels[pl.ds(1 - g, 1), :], (rows, rows)).T

    def terms(products, match):
        logits = factor * products + shift_bias
        turned = jnp.where(match, -logits, logits)
        small = jnp.exp(-jnp.abs(turned))
        sig = jnp.where(turned >= 0, 1.0, small) / (1.0 + small)
        loss = jnp.maximum(turned, 0.0) + jnp.log1p(small)
        loss = jnp.sum(loss.reshape(loss.shape[0] // 8, 8, rows), axis=0)
        return jnp.where(match, -sig, sig).astype(jnp.bfloat16), loss

    def first_id(slot):
        return lax.rem(b - slot + blocks, blocks) * (2 * rows)

    own = images[pl.ds(0, rows)]

    def own_tile(slot):
        products = lax.dot_general(texts[slot], own, NT, preferred_element_type=jnp.float32)
        weights[slot], loss = terms(products, own_ids + first_id(slot) == own_labels)
        return loss

    total = own_tile(0)
    near, far = 1 + 2 * core, 3 - 2 * core
    rem_copy(text_hbm, texts.at[near], send.at[near], recv.at[near], mate).wait_recv()
    forward = rem_copy(texts.at[near], texts.at[2], send.at[2], recv.at[2], mate)
    forward.start()
    passes_on = (core == 0) & (x != 3)
    pass_on = rem_copy(texts.at[1], texts.at[3], send.at[4], recv.at[3], at(2))

    @pl.when(passes_on)
    def _():
        pass_on.start()

    total += own_tile(near)
    rem_copy(text_hbm, texts.at[far], send.at[far], recv.at[far], mate).wait_recv()
    total += own_tile(far)
    forward.wait_recv()
    total += own_tile(2)
    all_texts = texts[...].reshape(STEPS * rows, width)
    grad_image_ref[...] = lax.dot_general(
        weights[...].reshape(STEPS * rows, rows), all_texts, TN, preferred_element_type=jnp.float32)

    back = [rem_copy(out_other.at[pl.ds(c * part, part)], in_other.at[pl.ds(c * part, part)],
                     back_send.at[c], back_recv.at[c], partner) for c in range(CHUNKS)]
    z_copies = [rem_copy(loss_z.at[zr], loss_z.at[zr], z_send.at[i], z_recv.at[i], dev)
                for i, dev in enumerate(r_devs)]
    for c in range(CHUNKS):
        over[c].wait_recv()
        here = pl.ds(c * part, part)
        products = lax.dot_general(images[pl.ds(rows + c * part, part)], all_texts, NT,
                                   preferred_element_type=jnp.float32)
        for slot in range(STEPS):
            match = (other_ids[:part] + first_id(slot)) == other_labels[c * part:(c + 1) * part]
            there = pl.ds(slot * rows, rows)
            weights_other[here, there], loss = terms(products[:, slot * rows:(slot + 1) * rows], match)
            total += loss
        if c == CHUNKS - 1:
            loss_z[zr] = total
            for copy in z_copies:
                copy.start()
        out_other[here, :] = jnp.dot(
            weights_other[here, :], all_texts, preferred_element_type=jnp.float32).astype(jnp.bfloat16)
        back[c].start()

    def ordered(buffer, count):
        value = buffer[0]
        for i in range(1, count):
            value = value + buffer[i]
        return value

    def partial(slot):
        column = pl.ds(pl.multiple_of(slot * rows, rows), rows)
        return jnp.dot(weights[slot], own, preferred_element_type=jnp.float32) + lax.dot_general(
            weights_other[:, column], images[pl.ds(rows, rows)], TN, preferred_element_type=jnp.float32)

    mate_out[...] = partial(2).astype(jnp.bfloat16)
    to_mate = rem_copy(mate_out, mate_in, send.at[5], recv.at[5], mate)
    to_mate.start()
    ext_out[...] = partial(far).astype(jnp.bfloat16)
    to_ext = rem_copy(ext_out, ext_in, send.at[6], recv.at[6], at(2 * core - 3))
    ext_relay = rem_copy(ext_out, relay, send.at[6], recv.at[9], at(5))
    ext_by_relay = (core == 0) & first

    @pl.when(ext_by_relay)
    def _():
        ext_relay.start()

    @pl.when(jnp.logical_not(ext_by_relay))
    def _():
        to_ext.start()

    mine = partial(near)
    for c in z_copies:
        c.wait_recv()
    loss_q[zq] = ordered(loss_z, 4)

    @pl.when(zq != 1)
    def _():
        pl.semaphore_wait(token, 1)

    q_copies = [rem_copy(loss_q.at[zq], loss_q.at[zq], q_send.at[i], q_recv.at[i], dev)
                for i, dev in enumerate(q_devs)]
    for c in q_copies:
        c.start()

    to_mate.wait_recv()
    sum_out[...] = (mine + mate_in[...].astype(jnp.float32)).astype(jnp.bfloat16)
    to_sum = rem_copy(sum_out, sum_in, send.at[7], recv.at[7], at(-1 - 2 * core))
    sum_relay = rem_copy(sum_out, relay, send.at[7], recv.at[9], at(5))
    sum_by_relay = (core == 1) & first

    @pl.when(sum_by_relay)
    def _():
        sum_relay.start()

    @pl.when(jnp.logical_not(sum_by_relay))
    def _():
        to_sum.start()

    grad_text_ref[...] = partial(0)

    relays_sum = (core == 0) & last
    relays_ext = (core == 1) & (x == 2)
    relay_sum = rem_copy(relay, sum_in, send.at[9], recv.at[7], at(-8))
    relay_ext = rem_copy(relay, ext_in, send.at[9], recv.at[6], at(-8))

    @pl.when(relays_sum)
    def _():
        sum_relay.wait_recv()
        relay_sum.start()

    @pl.when(relays_ext)
    def _():
        ext_relay.wait_recv()
        relay_ext.start()

    for c in q_copies:
        c.wait_recv()
    loss_y[y] = ordered(loss_q, 3)
    y_copies = [rem_copy(loss_y.at[y], loss_y.at[y], y_send.at[i], y_recv.at[i], dev)
                for i, dev in enumerate(y_devs)]
    for c in y_copies:
        c.start()
    for c in back:
        c.wait_recv()
    grad_image_ref[...] = factor * (grad_image_ref[...] + in_other[...].astype(jnp.float32))
    for c in y_copies:
        c.wait_recv()
    loss_xc[xc_me] = ordered(loss_y, 8)
    xc_copies = [rem_copy(loss_xc.at[xc_me], loss_xc.at[xc_me], xc_send.at[i], xc_recv.at[i], dev)
                 for i, dev in enumerate(xc_devs)]
    for c in xc_copies:
        c.start()
    to_ext.wait_recv()
    to_sum.wait_recv()
    grad_text_ref[...] = factor * (
        grad_text_ref[...] + ext_in[...].astype(jnp.float32) + sum_in[...].astype(jnp.float32))
    for c in xc_copies:
        c.wait_recv()
    whole = jnp.sum(jnp.sum(ordered(loss_xc, 8), axis=1, keepdims=True), axis=0, keepdims=True)
    loss_ref[...] = whole / (blocks * 2 * rows)

    for c in [text_1, forward, to_mate, to_ext, to_sum] + over + back + xc_copies + y_copies + z_copies + q_copies:
        c.wait_send()

    @pl.when(direct | by_relay)
    def _():
        text_3.wait_send()

    @pl.when(relays_text)
    def _():
        relay_text.wait_send()

    @pl.when(passes_on)
    def _():
        pass_on.wait_send()

    @pl.when(relays_sum | relays_ext)
    def _():
        relay_sum.wait_send()


def body(image_embed, text_embed, pair_labels, logit_scale, logit_bias):
    rows, width = image_embed.shape
    shard = pltpu.VMEM((rows, width), jnp.bfloat16)
    dma = pltpu.SemaphoreType.DMA
    tiles = lambda n: pltpu.VMEM((n, 8, 128), jnp.float32)
    hbm = pl.BlockSpec(memory_space=pl.ANY)
    smem = pl.BlockSpec(memory_space=pltpu.SMEM)
    vmem = pl.BlockSpec(memory_space=pltpu.VMEM)
    grad = jax.ShapeDtypeStruct((rows, width), jnp.float32)
    in_hbm = lambda a: pltpu.with_memory_space_constraint(a, pltpu.HBM)
    mean_loss, grad_image, grad_text = pl.pallas_call(
        kernel,
        out_shape=(jax.ShapeDtypeStruct((1, 1), jnp.float32), grad, grad),
        in_specs=[hbm] * 3 + [smem] * 2,
        out_specs=(vmem, vmem, vmem),
        scratch_shapes=[
            pltpu.VMEM((2 * rows, width), jnp.bfloat16),
            pltpu.VMEM((STEPS, rows, width), jnp.bfloat16),
            pltpu.VMEM((2, rows), jnp.int32),
            pltpu.VMEM((STEPS, rows, rows), jnp.bfloat16),
            pltpu.VMEM((rows, STEPS * rows), jnp.bfloat16),
            shard, shard, shard, shard, shard, shard, shard, shard, shard,
            tiles(8), tiles(8), tiles(4), tiles(3),
            dma((10,)), dma((10,)), dma((CHUNKS,)), dma((CHUNKS,)), dma((CHUNKS,)), dma((CHUNKS,)), dma((3,)),
            dma((7,)), dma((7,)), dma((7,)), dma((7,)), dma((3,)), dma((3,)), dma((2,)), dma((2,)),
            pltpu.SemaphoreType.REGULAR,
        ],
        compiler_params=pltpu.CompilerParams(
            collective_id=0, has_side_effects=True, vmem_limit_bytes=40 * 2**20),
        cost_estimate=pl.CostEstimate(
            flops=6 * 2 * rows * STEPS * rows * width, bytes_accessed=8 * rows * width, transcendentals=0),
        name="band",
    )(in_hbm(image_embed), in_hbm(text_embed), in_hbm(pair_labels.reshape(2, rows)), logit_scale, logit_bias)
    return mean_loss.reshape(()), grad_image, grad_text


def solution(mesh):
    in_specs = (P(("blk", "grp"), None), P(("blk", "grp"), None), P("blk"), P(), P())
    out_specs = (P(), P(("blk", "grp"), None), P(("blk", "grp"), None))
    return jax.shard_map(body, mesh=mesh, in_specs=in_specs, out_specs=out_specs, check_vma=False)
```

```python
import math

import jax
import jax.numpy as jnp
from jax import lax
from jax.experimental import pallas as pl
from jax.experimental.pallas import tpu as pltpu
from jax.sharding import PartitionSpec as P

STEPS = 4
CHUNKS = 2
NT = (((1,), (1,)), ((), ()))
TN = (((0,), (0,)), ((), ()))


def rem_copy(src, dst, send, recv, dev):
    return pltpu.make_async_remote_copy(
        src_ref=src, dst_ref=dst, send_sem=send, recv_sem=recv, device_id=dev,
        device_id_type=pl.DeviceIdType.MESH)


def kernel(image_hbm, text_hbm, labels_hbm, scale_ref, bias_ref,
           loss_ref, grad_image_ref, grad_text_ref,
           images, texts, labels, weights, weights_other, relay, out_other, in_other, mate_out, mate_in,
           ext_out, ext_in, sum_out, sum_in, loss_xc, loss_y, loss_z,
           send, recv, over_send, over_recv, back_send, back_recv, local, xc_send, xc_recv, y_send, y_recv, z_send, z_recv, token):
    rows, width = image_hbm.shape
    blocks = lax.axis_size("blk")
    b = lax.axis_index("blk")
    g = lax.axis_index("grp")
    core = b % 2
    x = (b // 2) % 4
    y = g * 4 + (b // 8) % 4
    z = b // 32
    zq = z // 4
    zr = z % 4

    def at(k):
        return (lax.rem(b + k + blocks, blocks), g)

    def place(x, y, z, core):
        return (((z * 4 + y % 4) * 4 + x) * 2 + core, y // 4)

    partner = (b, 1 - g)
    mate = (b + 1 - 2 * core, g)
    xc_me = x * 2 + core
    xc_peers = [lax.rem(xc_me + i, 8) for i in range(1, 8)]
    y_peers = [lax.rem(y + i, 8) for i in range(1, 8)]
    r_peers = [lax.rem(zr + i, 4) for i in range(1, 4)]
    q_peers = [lax.rem(zq + i, 3) for i in range(1, 3)]
    xc_devs = [place(p // 2, y, z, p % 2) for p in xc_peers]
    y_devs = [place(x, p, z, core) for p in y_peers]
    r_devs = [place(x, y, zq * 4 + p, core) for p in r_peers]
    z_devs = [place(x, y, lax.rem(z + i, 12), core) for i in range(1, 12)]
    q_devs = [place(x, y, p * 4 + zr, core) for p in q_peers]

    barrier = pltpu.get_barrier_semaphore()
    greeted = [at(-k) for k in (1, 2, 3, 6, 8)] + [partner] + xc_devs + y_devs + r_devs
    for dev in greeted:
        pl.semaphore_signal(barrier, inc=1, device_id=dev)

    greeters = len(greeted) + jnp.where(zq == 1, 2, 1)
    for k in (1, 2, 3, 6, 8):
        greeters += jnp.where(b >= k, 1, 0)

        @pl.when(b + k < blocks)
        def _():
            pl.semaphore_signal(barrier, inc=1, device_id=at(k))

    @pl.when(zq == 1)
    def _():
        for dev in q_devs:
            pl.semaphore_signal(barrier, inc=1, device_id=dev)

    @pl.when(zq != 1)
    def _():
        pl.semaphore_signal(barrier, inc=1, device_id=place(x, y, 4 + zr, core))

    local_copies = [
        pltpu.make_async_copy(image_hbm, images.at[pl.ds(0, rows)], local.at[0]),
        pltpu.make_async_copy(text_hbm, texts.at[0], local.at[1]),
        pltpu.make_async_copy(labels_hbm, labels, local.at[2]),
    ]
    for c in local_copies:
        c.start()

    pl.semaphore_wait(barrier, greeters)

    first, last = x == 0, x == 3
    text_1 = rem_copy(text_hbm, texts.at[1], send.at[1], recv.at[1], at(1))
    text_3 = rem_copy(text_hbm, texts.at[3], send.at[3], recv.at[3], at(3))
    text_relay = rem_copy(text_hbm, relay, send.at[3], recv.at[8], at(-3))
    text_1.start()
    direct = ((core == 0) & (x != 3)) | ((core == 1) & (x == 2))
    by_relay = (core == 0) & last

    @pl.when(direct)
    def _():
        text_3.start()

    @pl.when(by_relay)
    def _():
        text_relay.start()

    part = rows // CHUNKS
    over = [rem_copy(image_hbm.at[pl.ds(c * part, part)], images.at[pl.ds(rows + c * part, part)],
                     over_send.at[c], over_recv.at[c], partner) for c in range(CHUNKS)]
    relays_text = (core == 1) & (x == 1)
    relay_text = rem_copy(relay, texts.at[3], send.at[8], recv.at[3], at(6))
    over[0].start()

    @pl.when(relays_text)
    def _():
        text_relay.wait_recv()
        relay_text.start()

    for c in over[1:]:
        c.start()

    @pl.when(zq == 1)
    def _():
        for dev in q_devs:
            pl.semaphore_signal(token.at[0], inc=1, device_id=dev)

    factor = scale_ref[0] / math.sqrt(width)
    shift_bias = bias_ref[0]
    for c in local_copies:
        c.wait()
    own_ids = lax.broadcasted_iota(jnp.int32, (rows, rows), 0) + g * rows
    other_ids = lax.broadcasted_iota(jnp.int32, (rows, rows), 1) + g * rows
    own_labels = labels[pl.ds(g, 1), :]
    other_labels = jnp.broadcast_to(labels[pl.ds(1 - g, 1), :], (rows, rows)).T

    def terms(products, match):
        logits = factor * products + shift_bias
        turned = jnp.where(match, -logits, logits)
        small = jnp.exp(-jnp.abs(turned))
        sig = jnp.where(turned >= 0, 1.0, small) / (1.0 + small)
        loss = jnp.maximum(turned, 0.0) + jnp.log1p(small)
        loss = jnp.sum(loss.reshape(loss.shape[0] // 8, 8, rows), axis=0)
        return jnp.where(match, -sig, sig).astype(jnp.bfloat16), loss

    def first_id(slot):
        return lax.rem(b - slot + blocks, blocks) * (2 * rows)

    own = images[pl.ds(0, rows)]

    def own_tile(slot):
        products = lax.dot_general(texts[slot], own, NT, preferred_element_type=jnp.float32)
        weights[slot], loss = terms(products, own_ids + first_id(slot) == own_labels)
        return loss

    total = own_tile(0)
    near, far = 1 + 2 * core, 3 - 2 * core
    rem_copy(text_hbm, texts.at[near], send.at[near], recv.at[near], mate).wait_recv()
    forward = rem_copy(texts.at[near], texts.at[2], send.at[2], recv.at[2], mate)
    forward.start()
    passes_on = (core == 0) & (x != 3)
    pass_on = rem_copy(texts.at[1], texts.at[3], send.at[4], recv.at[3], at(2))

    @pl.when(passes_on)
    def _():
        pass_on.start()

    @pl.when(zq != 1)
    def _():
        pl.semaphore_wait(token.at[0], 1)
        for dev in q_devs:
            pl.semaphore_signal(token.at[1], inc=1, device_id=dev)

    total += own_tile(near)
    rem_copy(text_hbm, texts.at[far], send.at[far], recv.at[far], mate).wait_recv()
    total += own_tile(far)
    forward.wait_recv()
    total += own_tile(2)
    all_texts = texts[...].reshape(STEPS * rows, width)
    grad_image_ref[...] = lax.dot_general(
        weights[...].reshape(STEPS * rows, rows), all_texts, TN, preferred_element_type=jnp.float32)

    back = [rem_copy(out_other.at[pl.ds(c * part, part)], in_other.at[pl.ds(c * part, part)],
                     back_send.at[c], back_recv.at[c], partner) for c in range(CHUNKS)]
    z_copies = [rem_copy(loss_z.at[z], loss_z.at[z], z_send.at[i], z_recv.at[i], dev)
                for i, dev in enumerate(z_devs)]
    for c in range(CHUNKS):
        over[c].wait_recv()
        here = pl.ds(c * part, part)
        products = lax.dot_general(images[pl.ds(rows + c * part, part)], all_texts, NT,
                                   preferred_element_type=jnp.float32)
        for slot in range(STEPS):
            match = (other_ids[:part] + first_id(slot)) == other_labels[c * part:(c + 1) * part]
            there = pl.ds(slot * rows, rows)
            weights_other[here, there], loss = terms(products[:, slot * rows:(slot + 1) * rows], match)
            total += loss
        if c == CHUNKS - 1:
            loss_z[z] = total
            pl.semaphore_wait(token.at[1], jnp.where(zq == 1, 2, 1))
            for copy in z_copies:
                copy.start()
        out_other[here, :] = jnp.dot(
            weights_other[here, :], all_texts, preferred_element_type=jnp.float32).astype(jnp.bfloat16)
        back[c].start()

    def ordered(buffer, count):
        value = buffer[0]
        for i in range(1, count):
            value = value + buffer[i]
        return value

    def partial(slot):
        column = pl.ds(pl.multiple_of(slot * rows, rows), rows)
        return jnp.dot(weights[slot], own, preferred_element_type=jnp.float32) + lax.dot_general(
            weights_other[:, column], images[pl.ds(rows, rows)], TN, preferred_element_type=jnp.float32)

    mate_out[...] = partial(2).astype(jnp.bfloat16)
    to_mate = rem_copy(mate_out, mate_in, send.at[5], recv.at[5], mate)
    to_mate.start()
    ext_out[...] = partial(far).astype(jnp.bfloat16)
    to_ext = rem_copy(ext_out, ext_in, send.at[6], recv.at[6], at(2 * core - 3))
    ext_relay = rem_copy(ext_out, relay, send.at[6], recv.at[9], at(5))
    ext_by_relay = (core == 0) & first

    @pl.when(ext_by_relay)
    def _():
        ext_relay.start()

    @pl.when(jnp.logical_not(ext_by_relay))
    def _():
        to_ext.start()

    mine = partial(near)
    to_mate.wait_recv()
    sum_out[...] = (mine + mate_in[...].astype(jnp.float32)).astype(jnp.bfloat16)
    to_sum = rem_copy(sum_out, sum_in, send.at[7], recv.at[7], at(-1 - 2 * core))
    sum_relay = rem_copy(sum_out, relay, send.at[7], recv.at[9], at(5))
    sum_by_relay = (core == 1) & first

    @pl.when(sum_by_relay)
    def _():
        sum_relay.start()

    @pl.when(jnp.logical_not(sum_by_relay))
    def _():
        to_sum.start()

    grad_text_ref[...] = partial(0)

    relays_sum = (core == 0) & last
    relays_ext = (core == 1) & (x == 2)
    relay_sum = rem_copy(relay, sum_in, send.at[9], recv.at[7], at(-8))
    relay_ext = rem_copy(relay, ext_in, send.at[9], recv.at[6], at(-8))

    @pl.when(relays_sum)
    def _():
        sum_relay.wait_recv()
        relay_sum.start()

    @pl.when(relays_ext)
    def _():
        ext_relay.wait_recv()
        relay_ext.start()

    for c in z_copies:
        c.wait_recv()
    loss_y[y] = ordered(loss_z, 12)
    y_copies = [rem_copy(loss_y.at[y], loss_y.at[y], y_send.at[i], y_recv.at[i], dev)
                for i, dev in enumerate(y_devs)]
    for c in y_copies:
        c.start()
    for c in back:
        c.wait_recv()
    grad_image_ref[...] = factor * (grad_image_ref[...] + in_other[...].astype(jnp.float32))
    for c in y_copies:
        c.wait_recv()
    loss_xc[xc_me] = ordered(loss_y, 8)
    xc_copies = [rem_copy(loss_xc.at[xc_me], loss_xc.at[xc_me], xc_send.at[i], xc_recv.at[i], dev)
                 for i, dev in enumerate(xc_devs)]
    for c in xc_copies:
        c.start()
    to_ext.wait_recv()
    to_sum.wait_recv()
    grad_text_ref[...] = factor * (
        grad_text_ref[...] + ext_in[...].astype(jnp.float32) + sum_in[...].astype(jnp.float32))
    for c in xc_copies:
        c.wait_recv()
    whole = jnp.sum(jnp.sum(ordered(loss_xc, 8), axis=1, keepdims=True), axis=0, keepdims=True)
    loss_ref[...] = whole / (blocks * 2 * rows)

    for c in [text_1, forward, to_mate, to_ext, to_sum] + over + back + xc_copies + y_copies + z_copies:
        c.wait_send()

    @pl.when(direct | by_relay)
    def _():
        text_3.wait_send()

    @pl.when(relays_text)
    def _():
        relay_text.wait_send()

    @pl.when(passes_on)
    def _():
        pass_on.wait_send()

    @pl.when(relays_sum | relays_ext)
    def _():
        relay_sum.wait_send()


def body(image_embed, text_embed, pair_labels, logit_scale, logit_bias):
    rows, width = image_embed.shape
    shard = pltpu.VMEM((rows, width), jnp.bfloat16)
    dma = pltpu.SemaphoreType.DMA
    tiles = lambda n: pltpu.VMEM((n, 8, 128), jnp.float32)
    hbm = pl.BlockSpec(memory_space=pl.ANY)
    smem = pl.BlockSpec(memory_space=pltpu.SMEM)
    vmem = pl.BlockSpec(memory_space=pltpu.VMEM)
    grad = jax.ShapeDtypeStruct((rows, width), jnp.float32)
    in_hbm = lambda a: pltpu.with_memory_space_constraint(a, pltpu.HBM)
    mean_loss, grad_image, grad_text = pl.pallas_call(
        kernel,
        out_shape=(jax.ShapeDtypeStruct((1, 1), jnp.float32), grad, grad),
        in_specs=[hbm] * 3 + [smem] * 2,
        out_specs=(vmem, vmem, vmem),
        scratch_shapes=[
            pltpu.VMEM((2 * rows, width), jnp.bfloat16),
            pltpu.VMEM((STEPS, rows, width), jnp.bfloat16),
            pltpu.VMEM((2, rows), jnp.int32),
            pltpu.VMEM((STEPS, rows, rows), jnp.bfloat16),
            pltpu.VMEM((rows, STEPS * rows), jnp.bfloat16),
            shard, shard, shard, shard, shard, shard, shard, shard, shard,
            tiles(8), tiles(8), tiles(12),
            dma((10,)), dma((10,)), dma((CHUNKS,)), dma((CHUNKS,)), dma((CHUNKS,)), dma((CHUNKS,)), dma((3,)),
            dma((7,)), dma((7,)), dma((7,)), dma((7,)), dma((11,)), dma((11,)),
            pltpu.SemaphoreType.REGULAR((2,)),
        ],
        compiler_params=pltpu.CompilerParams(
            collective_id=0, has_side_effects=True, vmem_limit_bytes=40 * 2**20),
        cost_estimate=pl.CostEstimate(
            flops=6 * 2 * rows * STEPS * rows * width, bytes_accessed=8 * rows * width, transcendentals=0),
        name="band",
    )(in_hbm(image_embed), in_hbm(text_embed), in_hbm(pair_labels.reshape(2, rows)), logit_scale, logit_bias)
    return mean_loss.reshape(()), grad_image, grad_text


def solution(mesh):
    in_specs = (P(("blk", "grp"), None), P(("blk", "grp"), None), P("blk"), P(), P())
    out_specs = (P(), P(("blk", "grp"), None), P(("blk", "grp"), None))
    return jax.shard_map(body, mesh=mesh, in_specs=in_specs, out_specs=out_specs, check_vma=False)
```

```python
import math

import jax
import jax.numpy as jnp
from jax import lax
from jax.experimental import pallas as pl
from jax.experimental.pallas import tpu as pltpu
from jax.sharding import PartitionSpec as P

STEPS = 4
CHUNKS = 1
NT = (((1,), (1,)), ((), ()))
TN = (((0,), (0,)), ((), ()))


def rem_copy(src, dst, send, recv, dev):
    return pltpu.make_async_remote_copy(
        src_ref=src, dst_ref=dst, send_sem=send, recv_sem=recv, device_id=dev,
        device_id_type=pl.DeviceIdType.MESH)


def kernel(image_hbm, text_hbm, labels_hbm, scale_ref, bias_ref,
           loss_ref, grad_image_ref, grad_text_ref,
           images, texts, labels, weights, weights_other, relay, out_other, in_other, mate_out, mate_in,
           ext_out, ext_in, sum_out, sum_in, loss_xc, loss_y, loss_z,
           send, recv, over_send, over_recv, back_send, back_recv, local, xc_send, xc_recv, y_send, y_recv, z_send, z_recv, token):
    rows, width = image_hbm.shape
    blocks = lax.axis_size("blk")
    b = lax.axis_index("blk")
    g = lax.axis_index("grp")
    core = b % 2
    x = (b // 2) % 4
    y = g * 4 + (b // 8) % 4
    z = b // 32
    zq = z // 4
    zr = z % 4

    def at(k):
        return (lax.rem(b + k + blocks, blocks), g)

    def place(x, y, z, core):
        return (((z * 4 + y % 4) * 4 + x) * 2 + core, y // 4)

    partner = (b, 1 - g)
    mate = (b + 1 - 2 * core, g)
    xc_me = x * 2 + core
    xc_peers = [lax.rem(xc_me + i, 8) for i in range(1, 8)]
    y_peers = [lax.rem(y + i, 8) for i in range(1, 8)]
    r_peers = [lax.rem(zr + i, 4) for i in range(1, 4)]
    q_peers = [lax.rem(zq + i, 3) for i in range(1, 3)]
    xc_devs = [place(p // 2, y, z, p % 2) for p in xc_peers]
    y_devs = [place(x, p, z, core) for p in y_peers]
    r_devs = [place(x, y, zq * 4 + p, core) for p in r_peers]
    z_devs = [place(x, y, lax.rem(z + i, 12), core) for i in range(1, 12)]
    q_devs = [place(x, y, p * 4 + zr, core) for p in q_peers]

    barrier = pltpu.get_barrier_semaphore()
    greeted = [partner] + xc_devs + y_devs + r_devs
    for dev in greeted:
        pl.semaphore_signal(barrier, inc=1, device_id=dev)

    head = (x == 0) & (core == 1)
    greeters = len(greeted) + jnp.where(zq == 1, 2, 1) + jnp.where((x > 0) & (core == 1), 1, 0)

    @pl.when(head)
    def _():
        for k in (2, 4, 6):
            pl.semaphore_signal(barrier, inc=1, device_id=at(-k))

    @pl.when(zq == 1)
    def _():
        for dev in q_devs:
            pl.semaphore_signal(barrier, inc=1, device_id=dev)

    @pl.when(zq != 1)
    def _():
        pl.semaphore_signal(barrier, inc=1, device_id=place(x, y, 4 + zr, core))

    local_copies = [
        pltpu.make_async_copy(image_hbm, images.at[pl.ds(0, rows)], local.at[0]),
        pltpu.make_async_copy(text_hbm, texts.at[0], local.at[1]),
        pltpu.make_async_copy(labels_hbm, labels, local.at[2]),
    ]
    for c in local_copies:
        c.start()

    pl.semaphore_wait(barrier, greeters)

    first, last = x == 0, x == 3
    crosses = last & (core == 1)
    one = jnp.where(crosses, 2, 1)
    text_1 = rem_copy(text_hbm, texts.at[one], send.at[1], recv.at[one], at(one))
    text_3 = rem_copy(text_hbm, texts.at[3], send.at[3], recv.at[3], at(3))
    text_relay = rem_copy(text_hbm, relay, send.at[3], recv.at[8], at(jnp.where(core == 0, -3, 4)))
    text_1.start()
    direct = (core == 0) & (x != 3)
    by_relay = ((core == 0) & last) | ((core == 1) & (x == 2))

    @pl.when(direct)
    def _():
        text_3.start()

    @pl.when(by_relay)
    def _():
        text_relay.start()

    part = rows // CHUNKS
    over = [rem_copy(image_hbm.at[pl.ds(c * part, part)], images.at[pl.ds(rows + c * part, part)],
                     over_send.at[c], over_recv.at[c], partner) for c in range(CHUNKS)]
    relays_text = (core == 1) & (x == 1)
    relay_text = rem_copy(relay, texts.at[3], send.at[8], recv.at[3], at(jnp.where(x == 1, 6, -1)))
    over[0].start()

    @pl.when(relays_text)
    def _():
        text_relay.wait_recv()
        relay_text.start()

    for c in over[1:]:
        c.start()

    @pl.when(zq == 1)
    def _():
        for dev in q_devs:
            pl.semaphore_signal(token.at[0], inc=1, device_id=dev)

    for c in local_copies:
        c.wait()
    factor = scale_ref[0] / math.sqrt(width)
    shift_bias = bias_ref[0]
    own_ids = lax.broadcasted_iota(jnp.int32, (rows, rows), 0) + g * rows
    other_ids = lax.broadcasted_iota(jnp.int32, (rows, rows), 1) + g * rows
    own_labels = labels[pl.ds(g, 1), :]
    other_labels = jnp.broadcast_to(labels[pl.ds(1 - g, 1), :], (rows, rows)).T

    def terms(products, match):
        logits = factor * products + shift_bias
        turned = jnp.where(match, -logits, logits)
        small = jnp.exp(-jnp.abs(turned))
        sig = jnp.where(turned >= 0, 1.0, small) / (1.0 + small)
        loss = jnp.maximum(turned, 0.0) + jnp.log1p(small)
        loss = jnp.sum(loss.reshape(loss.shape[0] // 8, 8, rows), axis=0)
        return jnp.where(match, -sig, sig).astype(jnp.bfloat16), loss

    def first_id(slot):
        return lax.rem(b - slot + blocks, blocks) * (2 * rows)

    own = images[pl.ds(0, rows)]

    def own_tile(slot):
        products = lax.dot_general(texts[slot], own, NT, preferred_element_type=jnp.float32)
        weights[slot], loss = terms(products, own_ids + first_id(slot) == own_labels)
        return loss

    total = own_tile(0)
    near, far = 1 + 2 * core, 3 - 2 * core
    def arrival(slot):
        return rem_copy(text_hbm, texts.at[slot], send.at[0], recv.at[slot], mate)

    next_slots = [jnp.where(first, jnp.where(core == 1, 2, 1), near),
                  jnp.where(first, 3, far),
                  jnp.where(head, 1, 2)]
    goes = jnp.where(head, 1, 2)
    forwards = jnp.logical_not(first & (core == 0))
    passes_on = ((core == 0) & ((x == 1) | (x == 2))) | head
    forward = rem_copy(texts.at[next_slots[0]], texts.at[goes], send.at[2], recv.at[goes], mate)
    pass_on = rem_copy(texts.at[next_slots[0]], texts.at[3], send.at[4], recv.at[3], at(jnp.where(core == 0, 2, 1)))
    forward_2 = rem_copy(texts.at[3], texts.at[2], send.at[0], recv.at[2], mate)
    arrival(next_slots[0]).wait_recv()

    @pl.when(forwards)
    def _():
        forward.start()

    @pl.when(passes_on)
    def _():
        pass_on.start()

    @pl.when(zq != 1)
    def _():
        pl.semaphore_wait(token.at[0], 1)
        for dev in q_devs:
            pl.semaphore_signal(token.at[1], inc=1, device_id=dev)

    @pl.when(head)
    def _():
        text_relay.wait_recv()
        relay_text.start()

    total += own_tile(next_slots[0])
    arrival(next_slots[1]).wait_recv()

    @pl.when(head)
    def _():
        forward_2.start()

    total += own_tile(next_slots[1])
    arrival(next_slots[2]).wait_recv()
    total += own_tile(next_slots[2])
    all_texts = texts[...].reshape(STEPS * rows, width)
    grad_image_ref[...] = lax.dot_general(
        weights[...].reshape(STEPS * rows, rows), all_texts, TN, preferred_element_type=jnp.float32)

    back = [rem_copy(out_other.at[pl.ds(c * part, part)], in_other.at[pl.ds(c * part, part)],
                     back_send.at[c], back_recv.at[c], partner) for c in range(CHUNKS)]
    z_copies = [rem_copy(loss_z.at[z], loss_z.at[z], z_send.at[i], z_recv.at[i], dev)
                for i, dev in enumerate(z_devs)]
    for c in range(CHUNKS):
        over[c].wait_recv()
        here = pl.ds(c * part, part)
        products = lax.dot_general(images[pl.ds(rows + c * part, part)], all_texts, NT,
                                   preferred_element_type=jnp.float32)
        for slot in range(STEPS):
            match = (other_ids[:part] + first_id(slot)) == other_labels[c * part:(c + 1) * part]
            there = pl.ds(slot * rows, rows)
            weights_other[here, there], loss = terms(products[:, slot * rows:(slot + 1) * rows], match)
            total += loss
        if c == CHUNKS - 1:
            loss_z[z] = total
            pl.semaphore_wait(token.at[1], jnp.where(zq == 1, 2, 1))
            for copy in z_copies:
                copy.start()
        out_other[here, :] = jnp.dot(
            weights_other[here, :], all_texts, preferred_element_type=jnp.float32).astype(jnp.bfloat16)
        back[c].start()

    def ordered(buffer, count):
        value = buffer[0]
        for i in range(1, count):
            value = value + buffer[i]
        return value

    def partial(slot):
        column = pl.ds(pl.multiple_of(slot * rows, rows), rows)
        return jnp.dot(weights[slot], own, preferred_element_type=jnp.float32) + lax.dot_general(
            weights_other[:, column], images[pl.ds(rows, rows)], TN, preferred_element_type=jnp.float32)

    mate_out[...] = partial(2).astype(jnp.bfloat16)
    to_mate = rem_copy(mate_out, mate_in, send.at[5], recv.at[5], mate)
    to_mate.start()
    ext_out[...] = partial(far).astype(jnp.bfloat16)
    to_ext = rem_copy(ext_out, ext_in, send.at[6], recv.at[6], at(2 * core - 3))
    ext_relay = rem_copy(ext_out, relay, send.at[6], recv.at[9], at(5))
    ext_by_relay = (core == 0) & first

    @pl.when(ext_by_relay)
    def _():
        ext_relay.start()

    @pl.when(jnp.logical_not(ext_by_relay))
    def _():
        to_ext.start()

    mine = partial(near)
    to_mate.wait_recv()
    sum_out[...] = (mine + mate_in[...].astype(jnp.float32)).astype(jnp.bfloat16)
    to_sum = rem_copy(sum_out, sum_in, send.at[7], recv.at[7], at(-1 - 2 * core))
    sum_relay = rem_copy(sum_out, relay, send.at[7], recv.at[9], at(5))
    sum_by_relay = (core == 1) & first

    @pl.when(sum_by_relay)
    def _():
        sum_relay.start()

    @pl.when(jnp.logical_not(sum_by_relay))
    def _():
        to_sum.start()

    grad_text_ref[...] = partial(0)

    relays_sum = (core == 0) & last
    relays_ext = (core == 1) & (x == 2)
    relay_sum = rem_copy(relay, sum_in, send.at[9], recv.at[7], at(-8))
    relay_ext = rem_copy(relay, ext_in, send.at[9], recv.at[6], at(-8))

    @pl.when(relays_sum)
    def _():
        sum_relay.wait_recv()
        relay_sum.start()

    @pl.when(relays_ext)
    def _():
        ext_relay.wait_recv()
        relay_ext.start()

    for c in z_copies:
        c.wait_recv()
    loss_y[y] = ordered(loss_z, 12)
    y_copies = [rem_copy(loss_y.at[y], loss_y.at[y], y_send.at[i], y_recv.at[i], dev)
                for i, dev in enumerate(y_devs)]
    for c in y_copies:
        c.start()
    for c in back:
        c.wait_recv()
    grad_image_ref[...] = factor * (grad_image_ref[...] + in_other[...].astype(jnp.float32))
    for c in y_copies:
        c.wait_recv()
    loss_xc[xc_me] = ordered(loss_y, 8)
    xc_copies = [rem_copy(loss_xc.at[xc_me], loss_xc.at[xc_me], xc_send.at[i], xc_recv.at[i], dev)
                 for i, dev in enumerate(xc_devs)]
    for c in xc_copies:
        c.start()
    to_ext.wait_recv()
    to_sum.wait_recv()
    grad_text_ref[...] = factor * (
        grad_text_ref[...] + ext_in[...].astype(jnp.float32) + sum_in[...].astype(jnp.float32))
    for c in xc_copies:
        c.wait_recv()
    whole = jnp.sum(jnp.sum(ordered(loss_xc, 8), axis=1, keepdims=True), axis=0, keepdims=True)
    loss_ref[...] = whole / (blocks * 2 * rows)

    for c in [text_1, to_mate, to_ext, to_sum] + over + back + xc_copies + y_copies + z_copies:
        c.wait_send()

    @pl.when(direct | by_relay)
    def _():
        text_3.wait_send()

    @pl.when(relays_text | head)
    def _():
        relay_text.wait_send()

    @pl.when(forwards)
    def _():
        forward.wait_send()

    @pl.when(head)
    def _():
        forward_2.wait_send()

    @pl.when(passes_on)
    def _():
        pass_on.wait_send()

    @pl.when(relays_sum | relays_ext)
    def _():
        relay_sum.wait_send()


def body(image_embed, text_embed, pair_labels, logit_scale, logit_bias):
    rows, width = image_embed.shape
    shard = pltpu.VMEM((rows, width), jnp.bfloat16)
    dma = pltpu.SemaphoreType.DMA
    tiles = lambda n: pltpu.VMEM((n, 8, 128), jnp.float32)
    hbm = pl.BlockSpec(memory_space=pl.ANY)
    smem = pl.BlockSpec(memory_space=pltpu.SMEM)
    vmem = pl.BlockSpec(memory_space=pltpu.VMEM)
    grad = jax.ShapeDtypeStruct((rows, width), jnp.float32)
    in_hbm = lambda a: pltpu.with_memory_space_constraint(a, pltpu.HBM)
    mean_loss, grad_image, grad_text = pl.pallas_call(
        kernel,
        out_shape=(jax.ShapeDtypeStruct((1, 1), jnp.float32), grad, grad),
        in_specs=[hbm] * 3 + [smem] * 2,
        out_specs=(vmem, vmem, vmem),
        scratch_shapes=[
            pltpu.VMEM((2 * rows, width), jnp.bfloat16),
            pltpu.VMEM((STEPS, rows, width), jnp.bfloat16),
            pltpu.VMEM((2, rows), jnp.int32),
            pltpu.VMEM((STEPS, rows, rows), jnp.bfloat16),
            pltpu.VMEM((rows, STEPS * rows), jnp.bfloat16),
            shard, shard, shard, shard, shard, shard, shard, shard, shard,
            tiles(8), tiles(8), tiles(12),
            dma((10,)), dma((10,)), dma((CHUNKS,)), dma((CHUNKS,)), dma((CHUNKS,)), dma((CHUNKS,)), dma((3,)),
            dma((7,)), dma((7,)), dma((7,)), dma((7,)), dma((11,)), dma((11,)),
            pltpu.SemaphoreType.REGULAR((2,)),
        ],
        compiler_params=pltpu.CompilerParams(
            collective_id=0, has_side_effects=True, vmem_limit_bytes=40 * 2**20),
        cost_estimate=pl.CostEstimate(
            flops=6 * 2 * rows * STEPS * rows * width, bytes_accessed=8 * rows * width, transcendentals=0),
        name="band",
    )(in_hbm(image_embed), in_hbm(text_embed), in_hbm(pair_labels.reshape(2, rows)),
      logit_scale, logit_bias)
    return mean_loss.reshape(()), grad_image, grad_text


def solution(mesh):
    in_specs = (P(("blk", "grp"), None), P(("blk", "grp"), None), P("blk"), P(), P())
    out_specs = (P(), P(("blk", "grp"), None), P(("blk", "grp"), None))
    return jax.shard_map(body, mesh=mesh, in_specs=in_specs, out_specs=out_specs, check_vma=False)
```

```python
import math

import jax
import jax.numpy as jnp
from jax import lax
from jax.experimental import pallas as pl
from jax.experimental.pallas import tpu as pltpu
from jax.sharding import PartitionSpec as P

STEPS = 4
CHUNKS = 2
NT = (((1,), (1,)), ((), ()))
TN = (((0,), (0,)), ((), ()))


def rem_copy(src, dst, send, recv, dev):
    return pltpu.make_async_remote_copy(
        src_ref=src, dst_ref=dst, send_sem=send, recv_sem=recv, device_id=dev,
        device_id_type=pl.DeviceIdType.MESH)


def kernel(image_hbm, text_hbm, labels_hbm, scale_ref, bias_ref,
           loss_ref, grad_image_ref, grad_text_ref,
           images, texts, labels, weights, weights_other, relay, out_other, in_other, mate_out, mate_in,
           ext_out, ext_in, sum_out, sum_in, loss_xc, loss_y, loss_z,
           send, recv, over_send, over_recv, back_send, back_recv, local, xc_send, xc_recv, y_send, y_recv, z_send, z_recv, token):
    rows, width = image_hbm.shape
    blocks = lax.axis_size("blk")
    b = lax.axis_index("blk")
    g = lax.axis_index("grp")
    core = b % 2
    x = (b // 2) % 4
    y = g * 4 + (b // 8) % 4
    z = b // 32
    zq = z // 4
    zr = z % 4

    def at(k):
        return (lax.rem(b + k + blocks, blocks), g)

    def place(x, y, z, core):
        return (((z * 4 + y % 4) * 4 + x) * 2 + core, y // 4)

    partner = (b, 1 - g)
    mate = (b + 1 - 2 * core, g)
    xc_me = x * 2 + core
    xc_peers = [lax.rem(xc_me + i, 8) for i in range(1, 8)]
    y_peers = [lax.rem(y + i, 8) for i in range(1, 8)]
    r_peers = [lax.rem(zr + i, 4) for i in range(1, 4)]
    q_peers = [lax.rem(zq + i, 3) for i in range(1, 3)]
    xc_devs = [place(p // 2, y, z, p % 2) for p in xc_peers]
    y_devs = [place(x, p, z, core) for p in y_peers]
    r_devs = [place(x, y, zq * 4 + p, core) for p in r_peers]
    z_devs = [place(x, y, lax.rem(z + i, 12), core) for i in range(1, 12)]
    q_devs = [place(x, y, p * 4 + zr, core) for p in q_peers]

    barrier = pltpu.get_barrier_semaphore()
    greeted = [partner] + xc_devs + y_devs + r_devs
    for dev in greeted:
        pl.semaphore_signal(barrier, inc=1, device_id=dev)

    head = (x == 0) & (core == 1)
    greeters = len(greeted) + jnp.where(zq == 1, 2, 1) + jnp.where((x > 0) & (core == 1), 1, 0)

    @pl.when(head)
    def _():
        for k in (2, 4, 6):
            pl.semaphore_signal(barrier, inc=1, device_id=at(-k))

    @pl.when(zq == 1)
    def _():
        for dev in q_devs:
            pl.semaphore_signal(barrier, inc=1, device_id=dev)

    @pl.when(zq != 1)
    def _():
        pl.semaphore_signal(barrier, inc=1, device_id=place(x, y, 4 + zr, core))

    local_copies = [
        pltpu.make_async_copy(image_hbm, images.at[pl.ds(0, rows)], local.at[0]),
        pltpu.make_async_copy(text_hbm, texts.at[0], local.at[1]),
        pltpu.make_async_copy(labels_hbm, labels, local.at[2]),
    ]
    for c in local_copies:
        c.start()

    pl.semaphore_wait(barrier, greeters)

    first, last = x == 0, x == 3
    crosses = last & (core == 1)
    one = jnp.where(crosses, 2, 1)
    text_1 = rem_copy(text_hbm, texts.at[one], send.at[1], recv.at[one], at(one))
    text_3 = rem_copy(text_hbm, texts.at[3], send.at[3], recv.at[3], at(3))
    text_relay = rem_copy(text_hbm, relay, send.at[3], recv.at[8], at(jnp.where(core == 0, -3, 4)))
    text_1.start()
    direct = (core == 0) & (x != 3)
    by_relay = ((core == 0) & last) | ((core == 1) & (x == 2))

    @pl.when(direct)
    def _():
        text_3.start()

    @pl.when(by_relay)
    def _():
        text_relay.start()

    part = rows // CHUNKS
    over = [rem_copy(image_hbm.at[pl.ds(c * part, part)], images.at[pl.ds(rows + c * part, part)],
                     over_send.at[c], over_recv.at[c], partner) for c in range(CHUNKS)]
    relays_text = (core == 1) & (x == 1)
    relay_text = rem_copy(relay, texts.at[3], send.at[8], recv.at[3], at(jnp.where(x == 1, 6, -1)))
    over[0].start()

    @pl.when(relays_text)
    def _():
        text_relay.wait_recv()
        relay_text.start()

    for c in over[1:]:
        c.start()

    @pl.when(zq == 1)
    def _():
        for dev in q_devs:
            pl.semaphore_signal(token.at[0], inc=1, device_id=dev)

    for c in local_copies:
        c.wait()
    factor = scale_ref[0] / math.sqrt(width)
    shift_bias = bias_ref[0]
    own_ids = lax.broadcasted_iota(jnp.int32, (rows, rows), 0) + g * rows
    other_ids = lax.broadcasted_iota(jnp.int32, (rows, rows), 1) + g * rows
    own_labels = labels[pl.ds(g, 1), :]
    other_labels = jnp.broadcast_to(labels[pl.ds(1 - g, 1), :], (rows, rows)).T

    def terms(products, match):
        logits = factor * products + shift_bias
        turned = jnp.where(match, -logits, logits)
        small = jnp.exp(-jnp.abs(turned))
        sig = jnp.where(turned >= 0, 1.0, small) / (1.0 + small)
        loss = jnp.maximum(turned, 0.0) + jnp.log1p(small)
        loss = jnp.sum(loss.reshape(loss.shape[0] // 8, 8, rows), axis=0)
        return jnp.where(match, -sig, sig).astype(jnp.bfloat16), loss

    def first_id(slot):
        return lax.rem(b - slot + blocks, blocks) * (2 * rows)

    own = images[pl.ds(0, rows)]

    def own_tile(slot):
        products = lax.dot_general(texts[slot], own, NT, preferred_element_type=jnp.float32)
        weights[slot], loss = terms(products, own_ids + first_id(slot) == own_labels)
        return loss

    total = own_tile(0)
    near, far = 1 + 2 * core, 3 - 2 * core
    def arrival(slot):
        return rem_copy(text_hbm, texts.at[slot], send.at[0], recv.at[slot], mate)

    next_slots = [jnp.where(first, jnp.where(core == 1, 2, 1), near),
                  jnp.where(first, 3, far),
                  jnp.where(head, 1, 2)]
    goes = jnp.where(head, 1, 2)
    forwards = jnp.logical_not(first & (core == 0))
    passes_on = ((core == 0) & ((x == 1) | (x == 2))) | head
    forward = rem_copy(texts.at[next_slots[0]], texts.at[goes], send.at[2], recv.at[goes], mate)
    pass_on = rem_copy(texts.at[next_slots[0]], texts.at[3], send.at[4], recv.at[3], at(jnp.where(core == 0, 2, 1)))
    forward_2 = rem_copy(texts.at[3], texts.at[2], send.at[0], recv.at[2], mate)
    arrival(next_slots[0]).wait_recv()

    @pl.when(forwards)
    def _():
        forward.start()

    @pl.when(passes_on)
    def _():
        pass_on.start()

    @pl.when(zq != 1)
    def _():
        pl.semaphore_wait(token.at[0], 1)
        for dev in q_devs:
            pl.semaphore_signal(token.at[1], inc=1, device_id=dev)

    @pl.when(head)
    def _():
        text_relay.wait_recv()
        relay_text.start()

    total += own_tile(next_slots[0])
    arrival(next_slots[1]).wait_recv()

    @pl.when(head)
    def _():
        forward_2.start()

    total += own_tile(next_slots[1])
    arrival(next_slots[2]).wait_recv()
    total += own_tile(next_slots[2])
    all_texts = texts[...].reshape(STEPS * rows, width)
    grad_image_ref[...] = lax.dot_general(
        weights[...].reshape(STEPS * rows, rows), all_texts, TN, preferred_element_type=jnp.float32)

    back = [rem_copy(out_other.at[pl.ds(c * part, part)], in_other.at[pl.ds(c * part, part)],
                     back_send.at[c], back_recv.at[c], partner) for c in range(CHUNKS)]
    z_copies = [rem_copy(loss_z.at[z], loss_z.at[z], z_send.at[i], z_recv.at[i], dev)
                for i, dev in enumerate(z_devs)]
    for c in range(CHUNKS):
        over[c].wait_recv()
        here = pl.ds(c * part, part)
        products = lax.dot_general(images[pl.ds(rows + c * part, part)], all_texts, NT,
                                   preferred_element_type=jnp.float32)
        for slot in range(STEPS):
            match = (other_ids[:part] + first_id(slot)) == other_labels[c * part:(c + 1) * part]
            there = pl.ds(slot * rows, rows)
            weights_other[here, there], loss = terms(products[:, slot * rows:(slot + 1) * rows], match)
            total += loss
        if c == CHUNKS - 1:
            loss_z[z] = total
            pl.semaphore_wait(token.at[1], jnp.where(zq == 1, 2, 1))
            for copy in z_copies:
                copy.start()
        out_other[here, :] = jnp.dot(
            weights_other[here, :], all_texts, preferred_element_type=jnp.float32).astype(jnp.bfloat16)

    for c in back:
        c.start()

    def ordered(buffer, count):
        value = buffer[0]
        for i in range(1, count):
            value = value + buffer[i]
        return value

    def partial(slot):
        column = pl.ds(pl.multiple_of(slot * rows, rows), rows)
        return jnp.dot(weights[slot], own, preferred_element_type=jnp.float32) + lax.dot_general(
            weights_other[:, column], images[pl.ds(rows, rows)], TN, preferred_element_type=jnp.float32)

    mate_out[...] = partial(2).astype(jnp.bfloat16)
    to_mate = rem_copy(mate_out, mate_in, send.at[5], recv.at[5], mate)
    to_mate.start()
    ext_out[...] = partial(far).astype(jnp.bfloat16)
    to_ext = rem_copy(ext_out, ext_in, send.at[6], recv.at[6], at(2 * core - 3))
    ext_relay = rem_copy(ext_out, relay, send.at[6], recv.at[9], at(5))
    ext_by_relay = (core == 0) & first

    @pl.when(ext_by_relay)
    def _():
        ext_relay.start()

    @pl.when(jnp.logical_not(ext_by_relay))
    def _():
        to_ext.start()

    mine = partial(near)
    to_mate.wait_recv()
    sum_out[...] = (mine + mate_in[...].astype(jnp.float32)).astype(jnp.bfloat16)
    to_sum = rem_copy(sum_out, sum_in, send.at[7], recv.at[7], at(-1 - 2 * core))
    sum_relay = rem_copy(sum_out, relay, send.at[7], recv.at[9], at(5))
    sum_by_relay = (core == 1) & first

    @pl.when(sum_by_relay)
    def _():
        sum_relay.start()

    @pl.when(jnp.logical_not(sum_by_relay))
    def _():
        to_sum.start()

    grad_text_ref[...] = partial(0)

    for c in z_copies:
        c.wait_recv()
    loss_y[y] = ordered(loss_z, 12)
    y_copies = [rem_copy(loss_y.at[y], loss_y.at[y], y_send.at[i], y_recv.at[i], dev)
                for i, dev in enumerate(y_devs)]
    for c in y_copies:
        c.start()

    relays_sum = (core == 0) & last
    relays_ext = (core == 1) & (x == 2)
    relay_sum = rem_copy(relay, sum_in, send.at[9], recv.at[7], at(-8))
    relay_ext = rem_copy(relay, ext_in, send.at[9], recv.at[6], at(-8))

    @pl.when(relays_sum)
    def _():
        sum_relay.wait_recv()
        relay_sum.start()

    @pl.when(relays_ext)
    def _():
        ext_relay.wait_recv()
        relay_ext.start()

    for c in back:
        c.wait_recv()
    grad_image_ref[...] = factor * (grad_image_ref[...] + in_other[...].astype(jnp.float32))
    for c in y_copies:
        c.wait_recv()
    loss_xc[xc_me] = ordered(loss_y, 8)
    xc_copies = [rem_copy(loss_xc.at[xc_me], loss_xc.at[xc_me], xc_send.at[i], xc_recv.at[i], dev)
                 for i, dev in enumerate(xc_devs)]
    for c in xc_copies:
        c.start()
    to_ext.wait_recv()
    to_sum.wait_recv()
    grad_text_ref[...] = factor * (
        grad_text_ref[...] + ext_in[...].astype(jnp.float32) + sum_in[...].astype(jnp.float32))
    for c in xc_copies:
        c.wait_recv()
    whole = jnp.sum(jnp.sum(ordered(loss_xc, 8), axis=1, keepdims=True), axis=0, keepdims=True)
    loss_ref[...] = whole / (blocks * 2 * rows)

    for c in [text_1, to_mate, to_ext, to_sum] + over + back + xc_copies + y_copies + z_copies:
        c.wait_send()

    @pl.when(direct | by_relay)
    def _():
        text_3.wait_send()

    @pl.when(relays_text | head)
    def _():
        relay_text.wait_send()

    @pl.when(forwards)
    def _():
        forward.wait_send()

    @pl.when(head)
    def _():
        forward_2.wait_send()

    @pl.when(passes_on)
    def _():
        pass_on.wait_send()

    @pl.when(relays_sum | relays_ext)
    def _():
        relay_sum.wait_send()


def hand_over(loss_in, image_in, text_in, loss_out, image_out, text_out, sems):
    copies = [pltpu.make_async_copy(a, o, sems.at[i]) for i, (a, o) in enumerate(
        [(image_in, image_out), (text_in, text_out), (loss_in, loss_out)])]
    for c in copies:
        c.start()
    for c in copies:
        c.wait()


def body(image_embed, text_embed, pair_labels, logit_scale, logit_bias):
    rows, width = image_embed.shape
    shard = pltpu.VMEM((rows, width), jnp.bfloat16)
    dma = pltpu.SemaphoreType.DMA
    tiles = lambda n: pltpu.VMEM((n, 8, 128), jnp.float32)
    hbm = pl.BlockSpec(memory_space=pl.ANY)
    smem = pl.BlockSpec(memory_space=pltpu.SMEM)
    vmem = pl.BlockSpec(memory_space=pltpu.VMEM)
    grad = jax.ShapeDtypeStruct((rows, width), jnp.float32)
    in_hbm = lambda a: pltpu.with_memory_space_constraint(a, pltpu.HBM)
    mean_loss, grad_image, grad_text = pl.pallas_call(
        kernel,
        out_shape=(jax.ShapeDtypeStruct((1, 1), jnp.float32), grad, grad),
        in_specs=[hbm] * 3 + [smem] * 2,
        out_specs=(vmem, vmem, vmem),
        scratch_shapes=[
            pltpu.VMEM((2 * rows, width), jnp.bfloat16),
            pltpu.VMEM((STEPS, rows, width), jnp.bfloat16),
            pltpu.VMEM((2, rows), jnp.int32),
            pltpu.VMEM((STEPS, rows, rows), jnp.bfloat16),
            pltpu.VMEM((rows, STEPS * rows), jnp.bfloat16),
            shard, shard, shard, shard, shard, shard, shard, shard, shard,
            tiles(8), tiles(8), tiles(12),
            dma((10,)), dma((10,)), dma((CHUNKS,)), dma((CHUNKS,)), dma((CHUNKS,)), dma((CHUNKS,)), dma((3,)),
            dma((7,)), dma((7,)), dma((7,)), dma((7,)), dma((11,)), dma((11,)),
            pltpu.SemaphoreType.REGULAR((2,)),
        ],
        compiler_params=pltpu.CompilerParams(
            collective_id=0, has_side_effects=True, vmem_limit_bytes=40 * 2**20),
        cost_estimate=pl.CostEstimate(
            flops=6 * 2 * rows * STEPS * rows * width, bytes_accessed=8 * rows * width, transcendentals=0),
        name="band",
    )(in_hbm(image_embed), in_hbm(text_embed), in_hbm(pair_labels.reshape(2, rows)),
      logit_scale, logit_bias)
    in_vmem = lambda a: pltpu.with_memory_space_constraint(a, pltpu.VMEM)
    mean_loss, grad_image, grad_text = pl.pallas_call(
        hand_over,
        out_shape=(jax.ShapeDtypeStruct((1, 1), jnp.float32), grad, grad),
        in_specs=[hbm] * 3,
        out_specs=(hbm, hbm, hbm),
        scratch_shapes=[dma((3,))],
        name="hand_over",
    )(in_vmem(mean_loss), in_vmem(grad_image), in_vmem(grad_text))
    return mean_loss.reshape(()), grad_image, grad_text


def solution(mesh):
    in_specs = (P(("blk", "grp"), None), P(("blk", "grp"), None), P("blk"), P(), P())
    out_specs = (P(), P(("blk", "grp"), None), P(("blk", "grp"), None))
    return jax.shard_map(body, mesh=mesh, in_specs=in_specs, out_specs=out_specs, check_vma=False)
```

```python
import math

import jax
import jax.numpy as jnp
from jax import lax
from jax.experimental import pallas as pl
from jax.experimental.pallas import tpu as pltpu
from jax.sharding import PartitionSpec as P

STEPS = 4
CHUNKS = 2
NT = (((1,), (1,)), ((), ()))
TN = (((0,), (0,)), ((), ()))


def rem_copy(src, dst, send, recv, dev):
    return pltpu.make_async_remote_copy(
        src_ref=src, dst_ref=dst, send_sem=send, recv_sem=recv, device_id=dev,
        device_id_type=pl.DeviceIdType.MESH)


def kernel(image_hbm, text_hbm, labels_hbm, scale_ref, bias_ref,
           loss_ref, grad_image_ref, grad_text_ref,
           images, texts, labels, weights, weights_other, relay, out_other, in_other, mate_out, mate_in,
           ext_out, ext_in, sum_out, sum_in, loss_xc, loss_y, loss_z,
           send, recv, over_send, over_recv, back_send, back_recv, local, xc_send, xc_recv, y_send, y_recv, z_send, z_recv, token):
    rows, width = image_hbm.shape
    blocks = lax.axis_size("blk")
    b = lax.axis_index("blk")
    g = lax.axis_index("grp")
    core = b % 2
    x = (b // 2) % 4
    y = g * 4 + (b // 8) % 4
    z = b // 32
    zq = z // 4
    zr = z % 4

    def at(k):
        return (lax.rem(b + k + blocks, blocks), g)

    def place(x, y, z, core):
        return (((z * 4 + y % 4) * 4 + x) * 2 + core, y // 4)

    partner = (b, 1 - g)
    mate = (b + 1 - 2 * core, g)
    xc_me = x * 2 + core
    xc_peers = [lax.rem(xc_me + i, 8) for i in range(1, 8)]
    y_peers = [lax.rem(y + i, 8) for i in range(1, 8)]
    r_peers = [lax.rem(zr + i, 4) for i in range(1, 4)]
    q_peers = [lax.rem(zq + i, 3) for i in range(1, 3)]
    xc_devs = [place(p // 2, y, z, p % 2) for p in xc_peers]
    y_devs = [place(x, p, z, core) for p in y_peers]
    r_devs = [place(x, y, zq * 4 + p, core) for p in r_peers]
    z_devs = [place(x, y, lax.rem(z + i, 12), core) for i in range(1, 12)]
    q_devs = [place(x, y, p * 4 + zr, core) for p in q_peers]

    barrier = pltpu.get_barrier_semaphore()
    greeted = [partner] + xc_devs + y_devs + r_devs
    for dev in greeted:
        pl.semaphore_signal(barrier, inc=1, device_id=dev)

    head = (x == 0) & (core == 1)
    greeters = len(greeted) + jnp.where(zq == 1, 2, 1) + jnp.where((x > 0) & (core == 1), 1, 0)

    @pl.when(head)
    def _():
        for k in (2, 4, 6):
            pl.semaphore_signal(barrier, inc=1, device_id=at(-k))

    @pl.when(zq == 1)
    def _():
        for dev in q_devs:
            pl.semaphore_signal(barrier, inc=1, device_id=dev)

    @pl.when(zq != 1)
    def _():
        pl.semaphore_signal(barrier, inc=1, device_id=place(x, y, 4 + zr, core))

    local_copies = [
        pltpu.make_async_copy(image_hbm, images.at[pl.ds(0, rows)], local.at[0]),
        pltpu.make_async_copy(text_hbm, texts.at[0], local.at[1]),
        pltpu.make_async_copy(labels_hbm, labels, local.at[2]),
    ]
    for c in local_copies:
        c.start()

    pl.semaphore_wait(barrier, greeters)

    first, last = x == 0, x == 3
    crosses = last & (core == 1)
    one = jnp.where(crosses, 2, 1)
    text_1 = rem_copy(text_hbm, texts.at[one], send.at[1], recv.at[one], at(one))
    text_3 = rem_copy(text_hbm, texts.at[3], send.at[3], recv.at[3], at(3))
    text_relay = rem_copy(text_hbm, relay, send.at[3], recv.at[8], at(jnp.where(core == 0, -3, 4)))
    text_1.start()
    direct = (core == 0) & (x != 3)
    by_relay = ((core == 0) & last) | ((core == 1) & (x == 2))

    @pl.when(direct)
    def _():
        text_3.start()

    @pl.when(by_relay)
    def _():
        text_relay.start()

    part = rows // CHUNKS
    over = [rem_copy(image_hbm.at[pl.ds(c * part, part)], images.at[pl.ds(rows + c * part, part)],
                     over_send.at[c], over_recv.at[c], partner) for c in range(CHUNKS)]
    relays_text = (core == 1) & (x == 1)
    relay_text = rem_copy(relay, texts.at[3], send.at[8], recv.at[3], at(jnp.where(x == 1, 6, -1)))
    over[0].start()

    @pl.when(relays_text)
    def _():
        text_relay.wait_recv()
        relay_text.start()

    for c in over[1:]:
        c.start()

    @pl.when(zq == 1)
    def _():
        for dev in q_devs:
            pl.semaphore_signal(token.at[0], inc=1, device_id=dev)

    for c in local_copies:
        c.wait()
    factor = scale_ref[0] / math.sqrt(width)
    shift_bias = bias_ref[0]
    own_ids = lax.broadcasted_iota(jnp.int32, (rows, rows), 0) + g * rows
    other_ids = lax.broadcasted_iota(jnp.int32, (rows, rows), 1) + g * rows
    own_labels = labels[pl.ds(g, 1), :]
    other_labels = jnp.broadcast_to(labels[pl.ds(1 - g, 1), :], (rows, rows)).T

    def terms(products, match):
        logits = factor * products + shift_bias
        turned = jnp.where(match, -logits, logits)
        small = jnp.exp(-jnp.abs(turned))
        sig = jnp.where(turned >= 0, 1.0, small) / (1.0 + small)
        loss = jnp.maximum(turned, 0.0) + jnp.log1p(small)
        loss = jnp.sum(loss.reshape(loss.shape[0] // 8, 8, rows), axis=0)
        return jnp.where(match, -sig, sig).astype(jnp.bfloat16), loss

    def first_id(slot):
        return lax.rem(b - slot + blocks, blocks) * (2 * rows)

    own = images[pl.ds(0, rows)]

    def own_tile(slot):
        products = lax.dot_general(texts[slot], own, NT, preferred_element_type=jnp.float32)
        weights[slot], loss = terms(products, own_ids + first_id(slot) == own_labels)
        return loss

    total = own_tile(0)
    near, far = 1 + 2 * core, 3 - 2 * core
    def arrival(slot):
        return rem_copy(text_hbm, texts.at[slot], send.at[0], recv.at[slot], mate)

    next_slots = [jnp.where(first, jnp.where(core == 1, 2, 1), near),
                  jnp.where(first, 3, far),
                  jnp.where(head, 1, 2)]
    goes = jnp.where(head, 1, 2)
    forwards = jnp.logical_not(first & (core == 0))
    passes_on = ((core == 0) & ((x == 1) | (x == 2))) | head
    forward = rem_copy(texts.at[next_slots[0]], texts.at[goes], send.at[2], recv.at[goes], mate)
    pass_on = rem_copy(texts.at[next_slots[0]], texts.at[3], send.at[4], recv.at[3], at(jnp.where(core == 0, 2, 1)))
    forward_2 = rem_copy(texts.at[3], texts.at[2], send.at[0], recv.at[2], mate)
    arrival(next_slots[0]).wait_recv()

    @pl.when(forwards)
    def _():
        forward.start()

    @pl.when(passes_on)
    def _():
        pass_on.start()

    @pl.when(zq != 1)
    def _():
        pl.semaphore_wait(token.at[0], 1)
        for dev in q_devs:
            pl.semaphore_signal(token.at[1], inc=1, device_id=dev)

    @pl.when(head)
    def _():
        text_relay.wait_recv()
        relay_text.start()

    total += own_tile(next_slots[0])
    arrival(next_slots[1]).wait_recv()

    @pl.when(head)
    def _():
        forward_2.start()

    total += own_tile(next_slots[1])
    arrival(next_slots[2]).wait_recv()
    total += own_tile(next_slots[2])
    all_texts = texts[...].reshape(STEPS * rows, width)
    grad_image_ref[...] = lax.dot_general(
        weights[...].reshape(STEPS * rows, rows), all_texts, TN, preferred_element_type=jnp.float32)

    back = [rem_copy(out_other.at[pl.ds(c * part, part)], in_other.at[pl.ds(c * part, part)],
                     back_send.at[c], back_recv.at[c], partner) for c in range(CHUNKS)]
    xc_copies = [rem_copy(loss_xc.at[xc_me], loss_xc.at[xc_me], xc_send.at[i], xc_recv.at[i], dev)
                 for i, dev in enumerate(xc_devs)]
    for c in range(CHUNKS):
        over[c].wait_recv()
        here = pl.ds(c * part, part)
        products = lax.dot_general(images[pl.ds(rows + c * part, part)], all_texts, NT,
                                   preferred_element_type=jnp.float32)
        for slot in range(STEPS):
            match = (other_ids[:part] + first_id(slot)) == other_labels[c * part:(c + 1) * part]
            there = pl.ds(slot * rows, rows)
            weights_other[here, there], loss = terms(products[:, slot * rows:(slot + 1) * rows], match)
            total += loss
        if c == CHUNKS - 1:
            loss_xc[xc_me] = total
            for copy in xc_copies:
                copy.start()
        out_other[here, :] = jnp.dot(
            weights_other[here, :], all_texts, preferred_element_type=jnp.float32).astype(jnp.bfloat16)

    for c in back:
        c.start()

    def ordered(buffer, count):
        value = buffer[0]
        for i in range(1, count):
            value = value + buffer[i]
        return value

    def partial(slot):
        column = pl.ds(pl.multiple_of(slot * rows, rows), rows)
        return jnp.dot(weights[slot], own, preferred_element_type=jnp.float32) + lax.dot_general(
            weights_other[:, column], images[pl.ds(rows, rows)], TN, preferred_element_type=jnp.float32)

    mate_out[...] = partial(2).astype(jnp.bfloat16)
    to_mate = rem_copy(mate_out, mate_in, send.at[5], recv.at[5], mate)
    to_mate.start()
    ext_out[...] = partial(far).astype(jnp.bfloat16)
    to_ext = rem_copy(ext_out, ext_in, send.at[6], recv.at[6], at(2 * core - 3))
    ext_relay = rem_copy(ext_out, relay, send.at[6], recv.at[9], at(5))
    ext_by_relay = (core == 0) & first

    @pl.when(ext_by_relay)
    def _():
        ext_relay.start()

    @pl.when(jnp.logical_not(ext_by_relay))
    def _():
        to_ext.start()

    mine = partial(near)
    to_mate.wait_recv()
    sum_out[...] = (mine + mate_in[...].astype(jnp.float32)).astype(jnp.bfloat16)
    to_sum = rem_copy(sum_out, sum_in, send.at[7], recv.at[7], at(-1 - 2 * core))
    sum_relay = rem_copy(sum_out, relay, send.at[7], recv.at[9], at(5))
    sum_by_relay = (core == 1) & first

    @pl.when(sum_by_relay)
    def _():
        sum_relay.start()

    @pl.when(jnp.logical_not(sum_by_relay))
    def _():
        to_sum.start()

    for c in xc_copies:
        c.wait_recv()
    loss_z[z] = ordered(loss_xc, 8)
    pl.semaphore_wait(token.at[1], jnp.where(zq == 1, 2, 1))
    z_copies = [rem_copy(loss_z.at[z], loss_z.at[z], z_send.at[i], z_recv.at[i], dev)
                for i, dev in enumerate(z_devs)]
    for c in z_copies:
        c.start()

    grad_text_ref[...] = partial(0)

    for c in z_copies:
        c.wait_recv()
    loss_y[y] = ordered(loss_z, 12)
    y_copies = [rem_copy(loss_y.at[y], loss_y.at[y], y_send.at[i], y_recv.at[i], dev)
                for i, dev in enumerate(y_devs)]
    for c in y_copies:
        c.start()

    relays_sum = (core == 0) & last
    relays_ext = (core == 1) & (x == 2)
    relay_sum = rem_copy(relay, sum_in, send.at[9], recv.at[7], at(-8))
    relay_ext = rem_copy(relay, ext_in, send.at[9], recv.at[6], at(-8))

    @pl.when(relays_sum)
    def _():
        sum_relay.wait_recv()
        relay_sum.start()

    @pl.when(relays_ext)
    def _():
        ext_relay.wait_recv()
        relay_ext.start()

    for c in back:
        c.wait_recv()
    grad_image_ref[...] = factor * (grad_image_ref[...] + in_other[...].astype(jnp.float32))
    to_ext.wait_recv()
    to_sum.wait_recv()
    grad_text_ref[...] = factor * (
        grad_text_ref[...] + ext_in[...].astype(jnp.float32) + sum_in[...].astype(jnp.float32))
    for c in y_copies:
        c.wait_recv()
    whole = jnp.sum(jnp.sum(ordered(loss_y, 8), axis=1, keepdims=True), axis=0, keepdims=True)
    loss_ref[...] = whole / (blocks * 2 * rows)

    for c in [text_1, to_mate, to_ext, to_sum] + over + back + xc_copies + y_copies + z_copies:
        c.wait_send()

    @pl.when(direct | by_relay)
    def _():
        text_3.wait_send()

    @pl.when(relays_text | head)
    def _():
        relay_text.wait_send()

    @pl.when(forwards)
    def _():
        forward.wait_send()

    @pl.when(head)
    def _():
        forward_2.wait_send()

    @pl.when(passes_on)
    def _():
        pass_on.wait_send()

    @pl.when(relays_sum | relays_ext)
    def _():
        relay_sum.wait_send()


def hand_over(loss_in, image_in, text_in, loss_out, image_out, text_out, sems):
    copies = [pltpu.make_async_copy(a, o, sems.at[i]) for i, (a, o) in enumerate(
        [(image_in, image_out), (text_in, text_out), (loss_in, loss_out)])]
    for c in copies:
        c.start()
    for c in copies:
        c.wait()


def body(image_embed, text_embed, pair_labels, logit_scale, logit_bias):
    rows, width = image_embed.shape
    shard = pltpu.VMEM((rows, width), jnp.bfloat16)
    dma = pltpu.SemaphoreType.DMA
    tiles = lambda n: pltpu.VMEM((n, 8, 128), jnp.float32)
    hbm = pl.BlockSpec(memory_space=pl.ANY)
    smem = pl.BlockSpec(memory_space=pltpu.SMEM)
    vmem = pl.BlockSpec(memory_space=pltpu.VMEM)
    grad = jax.ShapeDtypeStruct((rows, width), jnp.float32)
    in_hbm = lambda a: pltpu.with_memory_space_constraint(a, pltpu.HBM)
    mean_loss, grad_image, grad_text = pl.pallas_call(
        kernel,
        out_shape=(jax.ShapeDtypeStruct((1, 1), jnp.float32), grad, grad),
        in_specs=[hbm] * 3 + [smem] * 2,
        out_specs=(vmem, vmem, vmem),
        scratch_shapes=[
            pltpu.VMEM((2 * rows, width), jnp.bfloat16),
            pltpu.VMEM((STEPS, rows, width), jnp.bfloat16),
            pltpu.VMEM((2, rows), jnp.int32),
            pltpu.VMEM((STEPS, rows, rows), jnp.bfloat16),
            pltpu.VMEM((rows, STEPS * rows), jnp.bfloat16),
            shard, shard, shard, shard, shard, shard, shard, shard, shard,
            tiles(8), tiles(8), tiles(12),
            dma((10,)), dma((10,)), dma((CHUNKS,)), dma((CHUNKS,)), dma((CHUNKS,)), dma((CHUNKS,)), dma((3,)),
            dma((7,)), dma((7,)), dma((7,)), dma((7,)), dma((11,)), dma((11,)),
            pltpu.SemaphoreType.REGULAR((2,)),
        ],
        compiler_params=pltpu.CompilerParams(
            collective_id=0, has_side_effects=True, vmem_limit_bytes=40 * 2**20),
        cost_estimate=pl.CostEstimate(
            flops=6 * 2 * rows * STEPS * rows * width, bytes_accessed=8 * rows * width, transcendentals=0),
        name="band",
    )(in_hbm(image_embed), in_hbm(text_embed), in_hbm(pair_labels.reshape(2, rows)),
      logit_scale, logit_bias)
    in_vmem = lambda a: pltpu.with_memory_space_constraint(a, pltpu.VMEM)
    mean_loss, grad_image, grad_text = pl.pallas_call(
        hand_over,
        out_shape=(jax.ShapeDtypeStruct((1, 1), jnp.float32), grad, grad),
        in_specs=[hbm] * 3,
        out_specs=(hbm, hbm, hbm),
        scratch_shapes=[dma((3,))],
        name="hand_over",
    )(in_vmem(mean_loss), in_vmem(grad_image), in_vmem(grad_text))
    return mean_loss.reshape(()), grad_image, grad_text


def solution(mesh):
    in_specs = (P(("blk", "grp"), None), P(("blk", "grp"), None), P("blk"), P(), P())
    out_specs = (P(), P(("blk", "grp"), None), P(("blk", "grp"), None))
    return jax.shard_map(body, mesh=mesh, in_specs=in_specs, out_specs=out_specs, check_vma=False)
```

```python
import math

import jax
import jax.numpy as jnp
from jax import lax
from jax.experimental import pallas as pl
from jax.experimental.pallas import tpu as pltpu
from jax.sharding import PartitionSpec as P

STEPS = 4
CHUNKS = 2
NT = (((1,), (1,)), ((), ()))
TN = (((0,), (0,)), ((), ()))


def rem_copy(src, dst, send, recv, dev):
    return pltpu.make_async_remote_copy(
        src_ref=src, dst_ref=dst, send_sem=send, recv_sem=recv, device_id=dev,
        device_id_type=pl.DeviceIdType.MESH)


def kernel(image_hbm, text_hbm, labels_hbm, scale_ref, bias_ref,
           loss_ref, grad_image_ref, grad_text_ref,
           images, texts, labels, weights, weights_other, relay, out_other, in_other, mate_out, mate_in,
           ext_out, ext_in, sum_out, sum_in, loss_xc, loss_y, loss_z,
           send, recv, over_send, over_recv, back_send, back_recv, local, xc_send, xc_recv, y_send, y_recv, z_send, z_recv, token):
    rows, width = image_hbm.shape
    blocks = lax.axis_size("blk")
    b = lax.axis_index("blk")
    g = lax.axis_index("grp")
    core = b % 2
    x = (b // 2) % 4
    y = g * 4 + (b // 8) % 4
    z = b // 32
    zq = z // 4
    zr = z % 4

    def at(k):
        return (lax.rem(b + k + blocks, blocks), g)

    def place(x, y, z, core):
        return (((z * 4 + y % 4) * 4 + x) * 2 + core, y // 4)

    partner = (b, 1 - g)
    mate = (b + 1 - 2 * core, g)
    xc_me = x * 2 + core
    xc_peers = [lax.rem(xc_me + i, 8) for i in range(1, 8)]
    y_peers = [lax.rem(y + i, 8) for i in (4, 3, 5, 2, 6, 1, 7)]
    r_peers = [lax.rem(zr + i, 4) for i in range(1, 4)]
    q_peers = [lax.rem(zq + i, 3) for i in range(1, 3)]
    xc_devs = [place(p // 2, y, z, p % 2) for p in xc_peers]
    y_devs = [place(x, p, z, core) for p in y_peers]
    r_devs = [place(x, y, zq * 4 + p, core) for p in r_peers]
    z_devs = [place(x, y, lax.rem(z + i, 12), core) for i in range(1, 12)]
    q_devs = [place(x, y, p * 4 + zr, core) for p in q_peers]

    barrier = pltpu.get_barrier_semaphore()
    greeted = [partner] + xc_devs + y_devs + r_devs
    for dev in greeted:
        pl.semaphore_signal(barrier, inc=1, device_id=dev)

    head = (x == 0) & (core == 1)
    greeters = len(greeted) + jnp.where(zq == 1, 2, 1) + jnp.where((x > 0) & (core == 1), 1, 0)

    @pl.when(head)
    def _():
        for k in (2, 4, 6):
            pl.semaphore_signal(barrier, inc=1, device_id=at(-k))

    @pl.when(zq == 1)
    def _():
        for dev in q_devs:
            pl.semaphore_signal(barrier, inc=1, device_id=dev)

    @pl.when(zq != 1)
    def _():
        pl.semaphore_signal(barrier, inc=1, device_id=place(x, y, 4 + zr, core))

    local_copies = [
        pltpu.make_async_copy(image_hbm, images.at[pl.ds(0, rows)], local.at[0]),
        pltpu.make_async_copy(text_hbm, texts.at[0], local.at[1]),
        pltpu.make_async_copy(labels_hbm, labels, local.at[2]),
    ]
    for c in local_copies:
        c.start()

    pl.semaphore_wait(barrier, greeters)

    first, last = x == 0, x == 3
    crosses = last & (core == 1)
    one = jnp.where(crosses, 2, 1)
    text_1 = rem_copy(text_hbm, texts.at[one], send.at[1], recv.at[one], at(one))
    text_3 = rem_copy(text_hbm, texts.at[3], send.at[3], recv.at[3], at(3))
    text_relay = rem_copy(text_hbm, relay, send.at[3], recv.at[8], at(jnp.where(core == 0, -3, 4)))
    text_1.start()
    direct = (core == 0) & (x != 3)
    by_relay = ((core == 0) & last) | ((core == 1) & (x == 2))

    @pl.when(direct)
    def _():
        text_3.start()

    @pl.when(by_relay)
    def _():
        text_relay.start()

    part = rows // CHUNKS
    over = [rem_copy(image_hbm.at[pl.ds(c * part, part)], images.at[pl.ds(rows + c * part, part)],
                     over_send.at[c], over_recv.at[c], partner) for c in range(CHUNKS)]
    relays_text = (core == 1) & (x == 1)
    relay_text = rem_copy(relay, texts.at[3], send.at[8], recv.at[3], at(jnp.where(x == 1, 6, -1)))
    over[0].start()

    @pl.when(relays_text)
    def _():
        text_relay.wait_recv()
        relay_text.start()

    for c in over[1:]:
        c.start()

    @pl.when(zq == 1)
    def _():
        for dev in q_devs:
            pl.semaphore_signal(token.at[0], inc=1, device_id=dev)

    for c in local_copies:
        c.wait()
    factor = scale_ref[0] / math.sqrt(width)
    shift_bias = bias_ref[0]
    own_ids = lax.broadcasted_iota(jnp.int32, (rows, rows), 0) + g * rows
    other_ids = lax.broadcasted_iota(jnp.int32, (rows, rows), 1) + g * rows
    own_labels = labels[pl.ds(g, 1), :]
    other_labels = jnp.broadcast_to(labels[pl.ds(1 - g, 1), :], (rows, rows)).T

    def terms(products, match):
        logits = factor * products + shift_bias
        turned = jnp.where(match, -logits, logits)
        small = jnp.exp(-jnp.abs(turned))
        sig = jnp.where(turned >= 0, 1.0, small) / (1.0 + small)
        loss = jnp.maximum(turned, 0.0) + jnp.log1p(small)
        loss = jnp.sum(loss.reshape(loss.shape[0] // 8, 8, rows), axis=0)
        return jnp.where(match, -sig, sig).astype(jnp.bfloat16), loss

    def first_id(slot):
        return lax.rem(b - slot + blocks, blocks) * (2 * rows)

    own = images[pl.ds(0, rows)]

    def own_tile(slot):
        products = lax.dot_general(texts[slot], own, NT, preferred_element_type=jnp.float32)
        weights[slot], loss = terms(products, own_ids + first_id(slot) == own_labels)
        return loss

    total = own_tile(0)
    near, far = 1 + 2 * core, 3 - 2 * core
    def arrival(slot):
        return rem_copy(text_hbm, texts.at[slot], send.at[0], recv.at[slot], mate)

    next_slots = [jnp.where(first, jnp.where(core == 1, 2, 1), near),
                  jnp.where(first, 3, far),
                  jnp.where(head, 1, 2)]
    goes = jnp.where(head, 1, 2)
    forwards = jnp.logical_not(first & (core == 0))
    passes_on = ((core == 0) & ((x == 1) | (x == 2))) | head
    forward = rem_copy(texts.at[next_slots[0]], texts.at[goes], send.at[2], recv.at[goes], mate)
    pass_on = rem_copy(texts.at[next_slots[0]], texts.at[3], send.at[4], recv.at[3], at(jnp.where(core == 0, 2, 1)))
    forward_2 = rem_copy(texts.at[3], texts.at[2], send.at[0], recv.at[2], mate)
    arrival(next_slots[0]).wait_recv()

    @pl.when(forwards)
    def _():
        forward.start()

    @pl.when(passes_on)
    def _():
        pass_on.start()

    @pl.when(zq != 1)
    def _():
        pl.semaphore_wait(token.at[0], 1)
        for dev in q_devs:
            pl.semaphore_signal(token.at[1], inc=1, device_id=dev)

    @pl.when(head)
    def _():
        text_relay.wait_recv()
        relay_text.start()

    total += own_tile(next_slots[0])
    arrival(next_slots[1]).wait_recv()

    @pl.when(head)
    def _():
        forward_2.start()

    total += own_tile(next_slots[1])
    arrival(next_slots[2]).wait_recv()
    total += own_tile(next_slots[2])
    all_texts = texts[...].reshape(STEPS * rows, width)
    grad_image_ref[...] = lax.dot_general(
        weights[...].reshape(STEPS * rows, rows), all_texts, TN, preferred_element_type=jnp.float32)

    back = [rem_copy(out_other.at[pl.ds(c * part, part)], in_other.at[pl.ds(c * part, part)],
                     back_send.at[c], back_recv.at[c], partner) for c in range(CHUNKS)]
    xc_copies = [rem_copy(loss_xc.at[xc_me], loss_xc.at[xc_me], xc_send.at[i], xc_recv.at[i], dev)
                 for i, dev in enumerate(xc_devs)]
    for c in range(CHUNKS):
        over[c].wait_recv()
        here = pl.ds(c * part, part)
        products = lax.dot_general(images[pl.ds(rows + c * part, part)], all_texts, NT,
                                   preferred_element_type=jnp.float32)
        for slot in range(STEPS):
            match = (other_ids[:part] + first_id(slot)) == other_labels[c * part:(c + 1) * part]
            there = pl.ds(slot * rows, rows)
            weights_other[here, there], loss = terms(products[:, slot * rows:(slot + 1) * rows], match)
            total += loss
        if c == CHUNKS - 1:
            loss_xc[xc_me] = total
            for copy in xc_copies:
                copy.start()
        out_other[here, :] = jnp.dot(
            weights_other[here, :], all_texts, preferred_element_type=jnp.float32).astype(jnp.bfloat16)

    for c in back:
        c.start()

    def ordered(buffer, count):
        value = buffer[0]
        for i in range(1, count):
            value = value + buffer[i]
        return value

    def partial(slot):
        column = pl.ds(pl.multiple_of(slot * rows, rows), rows)
        return jnp.dot(weights[slot], own, preferred_element_type=jnp.float32) + lax.dot_general(
            weights_other[:, column], images[pl.ds(rows, rows)], TN, preferred_element_type=jnp.float32)

    mate_out[...] = partial(2).astype(jnp.bfloat16)
    to_mate = rem_copy(mate_out, mate_in, send.at[5], recv.at[5], mate)
    to_mate.start()
    ext_out[...] = partial(far).astype(jnp.bfloat16)
    to_ext = rem_copy(ext_out, ext_in, send.at[6], recv.at[6], at(2 * core - 3))
    ext_relay = rem_copy(ext_out, relay, send.at[6], recv.at[9], at(5))
    ext_by_relay = (core == 0) & first

    @pl.when(ext_by_relay)
    def _():
        ext_relay.start()

    @pl.when(jnp.logical_not(ext_by_relay))
    def _():
        to_ext.start()

    mine = partial(near)
    to_mate.wait_recv()
    sum_out[...] = (mine + mate_in[...].astype(jnp.float32)).astype(jnp.bfloat16)
    to_sum = rem_copy(sum_out, sum_in, send.at[7], recv.at[7], at(-1 - 2 * core))
    sum_relay = rem_copy(sum_out, relay, send.at[7], recv.at[9], at(5))
    sum_by_relay = (core == 1) & first

    @pl.when(sum_by_relay)
    def _():
        sum_relay.start()

    @pl.when(jnp.logical_not(sum_by_relay))
    def _():
        to_sum.start()

    for c in xc_copies:
        c.wait_recv()
    loss_z[z] = ordered(loss_xc, 8)
    pl.semaphore_wait(token.at[1], jnp.where(zq == 1, 2, 1))
    z_copies = [rem_copy(loss_z.at[z], loss_z.at[z], z_send.at[i], z_recv.at[i], dev)
                for i, dev in enumerate(z_devs)]
    for c in z_copies:
        c.start()

    grad_text_ref[...] = partial(0)

    for c in z_copies:
        c.wait_recv()
    loss_y[y] = ordered(loss_z, 12)
    y_copies = [rem_copy(loss_y.at[y], loss_y.at[y], y_send.at[i], y_recv.at[i], dev)
                for i, dev in enumerate(y_devs)]
    for c in y_copies:
        c.start()

    relays_sum = (core == 0) & last
    relays_ext = (core == 1) & (x == 2)
    relay_sum = rem_copy(relay, sum_in, send.at[9], recv.at[7], at(-8))
    relay_ext = rem_copy(relay, ext_in, send.at[9], recv.at[6], at(-8))

    @pl.when(relays_sum)
    def _():
        sum_relay.wait_recv()
        relay_sum.start()

    @pl.when(relays_ext)
    def _():
        ext_relay.wait_recv()
        relay_ext.start()

    for c in back:
        c.wait_recv()
    grad_image_ref[...] = factor * (grad_image_ref[...] + in_other[...].astype(jnp.float32))
    to_ext.wait_recv()
    to_sum.wait_recv()
    grad_text_ref[...] = factor * (
        grad_text_ref[...] + ext_in[...].astype(jnp.float32) + sum_in[...].astype(jnp.float32))
    for c in y_copies:
        c.wait_recv()
    whole = jnp.sum(jnp.sum(ordered(loss_y, 8), axis=1, keepdims=True), axis=0, keepdims=True)
    loss_ref[...] = whole / (blocks * 2 * rows)

    for c in [text_1, to_mate, to_ext, to_sum] + over + back + xc_copies + y_copies + z_copies:
        c.wait_send()

    @pl.when(direct | by_relay)
    def _():
        text_3.wait_send()

    @pl.when(relays_text | head)
    def _():
        relay_text.wait_send()

    @pl.when(forwards)
    def _():
        forward.wait_send()

    @pl.when(head)
    def _():
        forward_2.wait_send()

    @pl.when(passes_on)
    def _():
        pass_on.wait_send()

    @pl.when(relays_sum | relays_ext)
    def _():
        relay_sum.wait_send()


def hand_over(loss_in, image_in, text_in, loss_out, image_out, text_out, sems):
    copies = [pltpu.make_async_copy(a, o, sems.at[i]) for i, (a, o) in enumerate(
        [(image_in, image_out), (text_in, text_out), (loss_in, loss_out)])]
    for c in copies:
        c.start()
    for c in copies:
        c.wait()


def body(image_embed, text_embed, pair_labels, logit_scale, logit_bias):
    rows, width = image_embed.shape
    shard = pltpu.VMEM((rows, width), jnp.bfloat16)
    dma = pltpu.SemaphoreType.DMA
    tiles = lambda n: pltpu.VMEM((n, 8, 128), jnp.float32)
    hbm = pl.BlockSpec(memory_space=pl.ANY)
    smem = pl.BlockSpec(memory_space=pltpu.SMEM)
    vmem = pl.BlockSpec(memory_space=pltpu.VMEM)
    grad = jax.ShapeDtypeStruct((rows, width), jnp.float32)
    in_hbm = lambda a: pltpu.with_memory_space_constraint(a, pltpu.HBM)
    mean_loss, grad_image, grad_text = pl.pallas_call(
        kernel,
        out_shape=(jax.ShapeDtypeStruct((1, 1), jnp.float32), grad, grad),
        in_specs=[hbm] * 3 + [smem] * 2,
        out_specs=(vmem, vmem, vmem),
        scratch_shapes=[
            pltpu.VMEM((2 * rows, width), jnp.bfloat16),
            pltpu.VMEM((STEPS, rows, width), jnp.bfloat16),
            pltpu.VMEM((2, rows), jnp.int32),
            pltpu.VMEM((STEPS, rows, rows), jnp.bfloat16),
            pltpu.VMEM((rows, STEPS * rows), jnp.bfloat16),
            shard, shard, shard, shard, shard, shard, shard, shard, shard,
            tiles(8), tiles(8), tiles(12),
            dma((10,)), dma((10,)), dma((CHUNKS,)), dma((CHUNKS,)), dma((CHUNKS,)), dma((CHUNKS,)), dma((3,)),
            dma((7,)), dma((7,)), dma((7,)), dma((7,)), dma((11,)), dma((11,)),
            pltpu.SemaphoreType.REGULAR((2,)),
        ],
        compiler_params=pltpu.CompilerParams(
            collective_id=0, has_side_effects=True, vmem_limit_bytes=40 * 2**20),
        cost_estimate=pl.CostEstimate(
            flops=6 * 2 * rows * STEPS * rows * width, bytes_accessed=8 * rows * width, transcendentals=0),
        name="band",
    )(in_hbm(image_embed), in_hbm(text_embed), in_hbm(pair_labels.reshape(2, rows)),
      logit_scale, logit_bias)
    in_vmem = lambda a: pltpu.with_memory_space_constraint(a, pltpu.VMEM)
    mean_loss, grad_image, grad_text = pl.pallas_call(
        hand_over,
        out_shape=(jax.ShapeDtypeStruct((1, 1), jnp.float32), grad, grad),
        in_specs=[hbm] * 3,
        out_specs=(hbm, hbm, hbm),
        scratch_shapes=[dma((3,))],
        name="hand_over",
    )(in_vmem(mean_loss), in_vmem(grad_image), in_vmem(grad_text))
    return mean_loss.reshape(()), grad_image, grad_text


def solution(mesh):
    in_specs = (P(("blk", "grp"), None), P(("blk", "grp"), None), P("blk"), P(), P())
    out_specs = (P(), P(("blk", "grp"), None), P(("blk", "grp"), None))
    return jax.shard_map(body, mesh=mesh, in_specs=in_specs, out_specs=out_specs, check_vma=False)
```
